256 devices in a mesh: section: 4 (over x), lat: 32 (over y_hi, z, core), tok: 2 (over y_lo).
Axes of the slice: x: 4, y: 4 (y_hi: 2, y_lo: 2; y = y_hi * 2 + y_lo), z: 8, core: 2. Of those that a mesh axis runs over, the one named last changes fastest.
Arguments:
- residual: bfloat16 [2, 256, 8192], P('tok', 'section', 'lat'), may hold values from -6 to 6
- center: float32 [8192], P('lat'), may hold values from -5 to 5
- whiten: bfloat16 [8192, 8192], P('lat', 'section'), may hold values from -0.0625 to 0.0625
- decoder_bias: float32 [8192], P('section'), may hold values from -3 to 3
- encoder_weight: bfloat16 [8192, 32768], P(('section', 'tok'), 'lat'), may hold values from -0.0625 to 0.0625
- encoder_bias: float32 [32768], P('lat'), may hold values from -3 to 3
- decoder_weight: bfloat16 [32768, 8192], P('lat', ('section', 'tok')), may hold values from -0.75 to 0.75
- chosen: int32 [2, 256, 64], replicated, may hold values from 0 to 32767, as said below
Outputs:
- encoder_grad: bfloat16 [8192, 32768], P(('section', 'tok'), 'lat')
- decoder_grad: bfloat16 [32768, 8192], P('lat', ('section', 'tok'))
- bias_grad: float32 [32768], P(('lat', 'tok'))
The draws below stay inside these ranges and needn't reach their ends.
Inputs may be any that keep to these rules, and one draw needn't show every extreme that they name: `chosen`: each row names 64 different latents.
All inputs are finite; a program needn't handle non-finite values.
Results may differ from the reference program's by a relative error of at most 0.0083.
Values may be sent and summed in bfloat16 or wider, within the bound.
No kernel may reach another device: no remote copies, remote signals or barrier semaphores. Data moves between devices by JAX's collectives and lax.ppermute only.
A program may use at most 128 MiB of HBM per device.

```python
import jax
import jax.numpy as jnp
from jax import lax

D = 8192
ACTIVE_LATENTS = 64
ROWS = 256
LAT = 32768
N_TOK = 2


def draw_chosen(key, part):
    key = jax.random.fold_in(key, 7)
    shape = (N_TOK * ROWS, LAT)
    scores = jax.random.randint(key, shape, 0, 8192, dtype=jnp.int32)
    columns = lax.broadcasted_iota(jnp.int32, shape, 1)
    row_place = lax.broadcasted_iota(jnp.int32, shape, 0)
    ranked_scores = scores * LAT + columns
    forced_latents = (row_place == 0) & (columns == LAT - 1) | (row_place == 1) & (columns == 0)
    extra_score = jnp.where(forced_latents, 536870912, 0).astype(jnp.int32)
    picked_latents = lax.top_k(ranked_scores + extra_score, ACTIVE_LATENTS)[1]
    return picked_latents.astype(jnp.int32).reshape(N_TOK, ROWS, ACTIVE_LATENTS)


def steps_of(stream_key, shape, cuts, smallest, high):
    def one(dim, blocks):
        heights = jax.random.uniform(jax.random.fold_in(jax.random.fold_in(stream_key, 6), dim), (blocks,), jnp.float32, smallest / len(cuts), high / len(cuts))
        return jnp.repeat(jnp.exp(heights), shape[dim] // blocks).reshape((-1,) + (1,) * (len(shape) - dim - 1))

    gain = one(*cuts[0])
    for cut in cuts[1:]:
        gain = gain * one(*cut)
    return gain


def scatter_about(own_key, extent, scale, most, shards=(), kind=jnp.bfloat16):
    array = scale * jax.random.normal(own_key, extent, jnp.float32)
    if shards:
        array = array * steps_of(own_key, extent, shards, -0.22, 0.18)
    return jnp.clip(array, -most, most).astype(kind)


def setup_inputs(seed: int = 0) -> dict:
    seeds = jax.random.split(jax.random.key(seed), 9)
    residual = scatter_about(seeds[0], (N_TOK, ROWS, D), 1.0, 6.0, ((0, 2), (1, 4), (2, 32)))
    center = scatter_about(seeds[1], (D,), 1.0, 5.0, ((0, 32),), jnp.float32)
    whiten = scatter_about(seeds[2], (D, D), D ** -0.5, 0.0625, ((0, 32), (1, 4)))
    decoder_bias = scatter_about(seeds[3], (D,), 0.5, 3.0, ((0, 4),), jnp.float32)
    encoder_weight = scatter_about(seeds[4], (D, LAT), D ** -0.5, 0.0625, ((0, 8), (1, 32)))
    encoder_bias = scatter_about(seeds[5], (LAT,), 0.5, 3.0, ((0, 32),), jnp.float32)
    decoder_weight = scatter_about(seeds[6], (LAT, D), ACTIVE_LATENTS ** -0.5, 0.75, ((0, 32), (1, 8)))
    chosen = draw_chosen(jax.random.fold_in(seeds[8], 71), 0)
    return {"residual": residual, "center": center, "whiten": whiten, "decoder_bias": decoder_bias, "encoder_weight": encoder_weight, "encoder_bias": encoder_bias, "decoder_weight": decoder_weight, "chosen": chosen}


grad_scale = 0.125


def reference(residual, center, whiten, decoder_bias, encoder_weight, encoder_bias, decoder_weight, chosen):
    contract_rows = (((0,), (0,)), ((), ()))
    encoder_total = None
    decoder_total = None
    bias_total = None
    for member in range(N_TOK):
        centered = (residual[member].astype(jnp.float32) - center).astype(jnp.bfloat16)
        whitened = jnp.dot(centered, whiten, preferred_element_type=jnp.float32).astype(jnp.bfloat16)
        shifted = (whitened.astype(jnp.float32) - decoder_bias).astype(jnp.bfloat16)
        encoded = jnp.dot(shifted, encoder_weight, preferred_element_type=jnp.float32) + encoder_bias
        picked_latents = chosen[member].astype(jnp.int32)
        row_index = lax.broadcasted_iota(jnp.int32, picked_latents.shape, 0)
        selection = jnp.zeros(encoded.shape, jnp.float32).at[row_index, picked_latents].set(1.0)
        latent_codes = (encoded * selection).astype(jnp.bfloat16)
        rebuilt = jnp.dot(latent_codes, decoder_weight, preferred_element_type=jnp.float32) + decoder_bias
        residual_error = rebuilt - whitened.astype(jnp.float32)
        out_grad = (grad_scale * residual_error).astype(jnp.bfloat16)
        code_grad = lax.dot_general(out_grad, decoder_weight, (((1,), (1,)), ((), ())), preferred_element_type=jnp.float32)
        encoded_grad = (code_grad * selection).astype(jnp.bfloat16)
        encoder_part = lax.dot_general(shifted, encoded_grad, contract_rows, preferred_element_type=jnp.float32)
        decoder_part = lax.dot_general(latent_codes, out_grad, contract_rows, preferred_element_type=jnp.float32)
        bias_part = jnp.sum(encoded_grad.astype(jnp.float32), axis=0)
        if member == 0:
            encoder_total, decoder_total, bias_total = encoder_part, decoder_part, bias_part
        else:
            encoder_total = encoder_total + encoder_part
            decoder_total = decoder_total + decoder_part
            bias_total = bias_total + bias_part
    return encoder_total.astype(jnp.bfloat16), decoder_total.astype(jnp.bfloat16), bias_total
```

```python
import functools

import jax
import jax.numpy as jnp
from jax import lax
from jax.experimental import pallas as pl
from jax.experimental.pallas import tpu as pltpu
from jax.sharding import Mesh
from jax.sharding import PartitionSpec as P

grad_scale = 0.125
LANES = 128
F32 = jnp.float32
BF16 = jnp.bfloat16
WHOLE = pl.BlockSpec(memory_space=pltpu.VMEM)
PARAMS = pltpu.CompilerParams(vmem_limit_bytes=24 * 1024 * 1024)


def call(kernel, out_shape, operands, flops=0, moved=0):
    return pl.pallas_call(
        kernel,
        out_shape=out_shape,
        in_specs=[WHOLE] * len(operands),
        out_specs=jax.tree.map(lambda _: WHOLE, out_shape),
        compiler_params=PARAMS,
        cost_estimate=pl.CostEstimate(flops=flops, bytes_accessed=moved, transcendentals=0),
    )(*operands)


def find_kernel(place_ref, slot_ref):
    half = LANES // 2
    width = slot_ref.shape[2]

    def step(i, carry):
        rows = pl.ds(pl.multiple_of(i * 8, 8), 8)
        place = place_ref[rows, :]
        column = lax.broadcasted_iota(jnp.int32, (8, width), 1)
        for m in range(2):
            slot = jnp.full((8, width), -1, jnp.int32)
            for k in range(m * half, (m + 1) * half):
                slot = jnp.where(place[:, k : k + 1] == column, k, slot)
            slot_ref[m, rows, :] = slot
        return carry

    lax.fori_loop(0, place_ref.shape[0] // 8, step, 0)


def pick(y, place):
    lane, chunk = place & (LANES - 1), place >> 7
    out = jnp.zeros(place.shape, F32)
    for j in range(y.shape[1] // LANES):
        found = jnp.take_along_axis(y[:, j * LANES : (j + 1) * LANES], lane, axis=1)
        out = jnp.where(chunk == j, found, out)
    return out


def product_pick_kernel(contract, x_ref, w_ref, place_ref, out_ref):
    y = lax.dot_general(
        x_ref[...], w_ref[...], (((1,), (contract,)), ((), ())), preferred_element_type=F32
    )
    out_ref[...] = pick(y, place_ref[...])


def product_join_kernel(contract, x_ref, w_ref, place_ref, own_ref, out_ref):
    y = lax.dot_general(
        x_ref[...], w_ref[...], (((1,), (contract,)), ((), ())), preferred_element_type=F32
    )
    lane = lax.broadcasted_iota(jnp.int32, out_ref.shape, 1)
    mine = own_ref[...]
    out_ref[...] = jnp.where(lane < LANES // 2, mine, pick(y, place_ref[...])).astype(BF16)


def spread_codes_kernel(m, packed_ref, slot_ref, bias_ref, w_ref, codes_ref, part_ref):
    packed = packed_ref[...]
    for j in range(codes_ref.shape[1] // LANES):
        cols = pl.ds(j * LANES, LANES)
        slot = slot_ref[m, :, cols]
        value = jnp.take_along_axis(packed, jnp.maximum(slot, 0), axis=1) + bias_ref[:, cols]
        codes_ref[:, cols] = jnp.where(slot >= 0, value, 0.0).astype(BF16)
    part_ref[...] = jnp.dot(
        codes_ref[...], w_ref[...], preferred_element_type=F32
    ).astype(part_ref.dtype)


def spread_grad_kernel(packed_ref, slot_ref, grad_ref, total_ref):
    packed = packed_ref[...]
    rows = packed.shape[0]
    for j in range(grad_ref.shape[1] // LANES):
        cols = pl.ds(j * LANES, LANES)
        total = jnp.zeros((1, LANES), F32)
        for m in range(2):
            slot = slot_ref[m, :, cols]
            value = jnp.take_along_axis(packed, jnp.maximum(slot, 0), axis=1)
            grad = jnp.where(slot >= 0, value, 0.0).astype(BF16)
            grad_ref[m * rows : (m + 1) * rows, cols] = grad
            total = total + jnp.sum(grad.astype(F32), axis=0, keepdims=True)
        total_ref[:, cols] = total


def swap_cores(x):
    return lax.ppermute(x, "core", [(0, 1), (1, 0)])


def spread_out(x, axes):
    n = lax.axis_size(axes)
    return lax.all_to_all(jnp.broadcast_to(x[None], (n,) + x.shape), axes, 0, 0)


def sum_parts(x, axes):
    n = lax.axis_size(axes)
    parts = lax.all_to_all(x.reshape((n, x.shape[0] // n) + x.shape[1:]), axes, 0, 0)
    return jnp.sum(parts.astype(F32), axis=0)


FEATURES = ("section", "tok")
COLUMN = ("yh", "z")


def body(
    residual, center, whiten, decoder_bias, encoder_weight, encoder_bias, decoder_weight, chosen
):
    core = lax.axis_index("core")
    tok = lax.axis_index("tok")
    width = encoder_weight.shape[0]
    latents = encoder_bias.shape[0]
    first = ((lax.axis_index("yh") * 8 + lax.axis_index("z")) * 2 + core) * latents

    own_picks = lax.dynamic_index_in_dim(chosen, core, 0, keepdims=False)
    other_picks = lax.dynamic_index_in_dim(chosen, 1 - core, 0, keepdims=False)
    place = jnp.concatenate([own_picks, other_picks], axis=1).astype(jnp.int32) - first
    rows = place.shape[0]

    centered = (residual[0].astype(F32) - center).astype(BF16)
    arrived = spread_out(centered, ("tok", "section")).reshape(2, rows, -1)
    own_rows = lax.dynamic_index_in_dim(arrived, core, 0, keepdims=False)
    other_rows = lax.dynamic_index_in_dim(arrived, 1 - core, 0, keepdims=False)
    whiten_cols = lax.dynamic_slice_in_dim(whiten, tok * width, width, 1)
    bias_cols = lax.dynamic_slice_in_dim(decoder_bias, tok * width, width, 0)

    slot = call(
        find_kernel,
        jax.ShapeDtypeStruct((2, rows, latents), jnp.int32),
        (place,),
        flops=2 * 64 * 2 * rows * latents,
        moved=8 * rows * latents,
    )

    other_part = jnp.dot(other_rows, whiten_cols, preferred_element_type=F32).astype(BF16)
    from_core = swap_cores(other_part)
    own_part = jnp.dot(own_rows, whiten_cols, preferred_element_type=F32)
    whitened = sum_parts((own_part + from_core.astype(F32)).astype(BF16), COLUMN).astype(BF16)
    shifted_share = (whitened.astype(F32) - bias_cols).astype(BF16)
    own_shifted = spread_out(shifted_share, COLUMN).reshape(rows, width)
    other_shifted = swap_cores(own_shifted)

    flops = 2 * rows * width * latents
    moved = 2 * width * latents + 4 * rows * width
    packed_f32 = jax.ShapeDtypeStruct((rows, LANES), F32)
    packed_bf16 = jax.ShapeDtypeStruct((rows, LANES), BF16)

    def packed_product(contract, own, other, weight):
        mine = call(
            functools.partial(product_pick_kernel, contract),
            packed_f32,
            (own, weight, place),
            flops,
            moved,
        )
        both = call(
            functools.partial(product_join_kernel, contract),
            packed_bf16,
            (other, weight, place, mine),
            flops,
            moved,
        )
        share = sum_parts(both, FEATURES).astype(BF16)
        return spread_out(share, FEATURES).reshape(rows, LANES).astype(F32)

    encoded = packed_product(0, own_shifted, other_shifted, encoder_weight)

    def decode(m, kind):
        return call(
            functools.partial(spread_codes_kernel, m),
            (
                jax.ShapeDtypeStruct((rows, latents), BF16),
                jax.ShapeDtypeStruct((rows, width), kind),
            ),
            (encoded, slot, encoder_bias[None], decoder_weight),
            flops,
            moved,
        )

    other_codes, other_part = decode(1, BF16)
    from_core = swap_cores(other_part)
    own_codes, own_part = decode(0, F32)
    rebuilt = sum_parts((own_part + from_core.astype(F32)).astype(BF16), COLUMN) + bias_cols
    own_grad_share = (grad_scale * (rebuilt - whitened.astype(F32))).astype(BF16)
    own_grad = spread_out(own_grad_share, COLUMN).reshape(rows, width)
    other_grad = swap_cores(own_grad)

    code_grad = packed_product(1, own_grad, other_grad, decoder_weight)

    contract_rows = (((0,), (0,)), ((), ()))
    codes = jnp.concatenate([own_codes, other_codes], axis=0)
    out_grad = jnp.concatenate([own_grad, other_grad], axis=0)
    decoder_grad = lax.dot_general(
        codes, out_grad, contract_rows, preferred_element_type=F32
    ).astype(BF16)

    encoded_grad, bias_total = call(
        spread_grad_kernel,
        (
            jax.ShapeDtypeStruct((2 * rows, latents), BF16),
            jax.ShapeDtypeStruct((1, latents), F32),
        ),
        (code_grad, slot),
        0,
        12 * rows * latents,
    )
    shifted = jnp.concatenate([own_shifted, other_shifted], axis=0)
    encoder_grad = lax.dot_general(
        shifted, encoded_grad, contract_rows, preferred_element_type=F32
    ).astype(BF16)
    half = latents // 2
    bias_grad = lax.dynamic_slice_in_dim(bias_total[0], tok * half, half, 0)
    return encoder_grad, decoder_grad, bias_grad


def solution(mesh):
    fine = Mesh(mesh.devices.reshape(4, 2, 8, 2, 2), ("section", "yh", "z", "core", "tok"))
    lat = ("yh", "z", "core")
    return jax.shard_map(
        body,
        mesh=fine,
        in_specs=(
            P("tok", "section", lat),
            P(lat),
            P(lat, "section"),
            P("section"),
            P(("section", "tok"), lat),
            P(lat),
            P(lat, ("section", "tok")),
            P(),
        ),
        out_specs=(P(("section", "tok"), lat), P(lat, ("section", "tok")), P(lat + ("tok",))),
        check_vma=False,
    )
```

```python
import functools

import jax
import jax.numpy as jnp
from jax import lax
from jax.experimental import pallas as pl
from jax.experimental.pallas import tpu as pltpu
from jax.sharding import Mesh
from jax.sharding import PartitionSpec as P

grad_scale = 0.125
LANES = 128
F32 = jnp.float32
BF16 = jnp.bfloat16
WHOLE = pl.BlockSpec(memory_space=pltpu.VMEM)
PARAMS = pltpu.CompilerParams(vmem_limit_bytes=20 * 1024 * 1024)


def call(kernel, out_shape, operands, flops=0, moved=0):
    return pl.pallas_call(
        kernel,
        out_shape=out_shape,
        in_specs=[WHOLE] * len(operands),
        out_specs=jax.tree.map(lambda _: WHOLE, out_shape),
        compiler_params=PARAMS,
        cost_estimate=pl.CostEstimate(flops=flops, bytes_accessed=moved, transcendentals=0),
    )(*operands)


def find_kernel(place_ref, slot_ref):
    half = LANES // 2
    width = slot_ref.shape[2]

    def step(i, carry):
        rows = pl.ds(pl.multiple_of(i * 8, 8), 8)
        place = place_ref[rows, :]
        column = lax.broadcasted_iota(jnp.int32, (8, width), 1)
        for m in range(2):
            slot = jnp.full((8, width), -1, jnp.int32)
            for k in range(m * half, (m + 1) * half):
                slot = jnp.where(place[:, k : k + 1] == column, k, slot)
            slot_ref[m, rows, :] = slot
        return carry

    lax.fori_loop(0, place_ref.shape[0] // 8, step, 0)


def pick(y, place):
    lane, chunk = place & (LANES - 1), place >> 7
    out = jnp.zeros(place.shape, F32)
    for j in range(y.shape[1] // LANES):
        found = jnp.take_along_axis(y[:, j * LANES : (j + 1) * LANES], lane, axis=1)
        out = jnp.where(chunk == j, found, out)
    return out


def whiten_other_kernel(x_ref, center_ref, w_ref, out_ref):
    x = (x_ref[...].astype(F32) - center_ref[...]).astype(BF16)
    out_ref[...] = jnp.dot(x, w_ref[...], preferred_element_type=F32).astype(BF16)


def whiten_own_kernel(x_ref, center_ref, w_ref, add_ref, out_ref):
    x = (x_ref[...].astype(F32) - center_ref[...]).astype(BF16)
    y = jnp.dot(x, w_ref[...], preferred_element_type=F32) + add_ref[...].astype(F32)
    out_ref[...] = y.astype(BF16)


def shift_kernel(parts_ref, bias_ref, white_ref, out_ref):
    total = parts_ref[0].astype(F32)
    for i in range(1, parts_ref.shape[0]):
        total = total + parts_ref[i].astype(F32)
    white = total.astype(BF16)
    white_ref[...] = white
    shifted = (white.astype(F32) - bias_ref[...]).astype(BF16)
    for i in range(out_ref.shape[0]):
        out_ref[i] = shifted


def error_kernel(parts_ref, bias_ref, white_ref, out_ref):
    total = parts_ref[0].astype(F32)
    for i in range(1, parts_ref.shape[0]):
        total = total + parts_ref[i].astype(F32)
    error = (total + bias_ref[...]) - white_ref[...].astype(F32)
    grad = (grad_scale * error).astype(BF16)
    for i in range(out_ref.shape[0]):
        out_ref[i] = grad


def product_pick_kernel(contract, x_ref, w_ref, place_ref, out_ref):
    y = lax.dot_general(
        x_ref[...], w_ref[...], (((1,), (contract,)), ((), ())), preferred_element_type=F32
    )
    out_ref[...] = pick(y, place_ref[...])


def product_join_kernel(contract, x_ref, w_ref, place_ref, own_ref, out_ref):
    y = lax.dot_general(
        x_ref[...], w_ref[...], (((1,), (contract,)), ((), ())), preferred_element_type=F32
    )
    lane = lax.broadcasted_iota(jnp.int32, own_ref.shape, 1)
    both = jnp.where(lane < LANES // 2, own_ref[...], pick(y, place_ref[...])).astype(BF16)
    for i in range(out_ref.shape[0]):
        out_ref[i] = both


def packed_sum(parts_ref):
    total = parts_ref[0].astype(F32)
    for i in range(1, parts_ref.shape[0]):
        total = total + parts_ref[i].astype(F32)
    return total


def spread_codes(m, packed_ref, slot_ref, bias_ref, codes_ref):
    packed = packed_sum(packed_ref)
    for j in range(codes_ref.shape[1] // LANES):
        cols = pl.ds(j * LANES, LANES)
        slot = slot_ref[m, :, cols]
        value = jnp.take_along_axis(packed, jnp.maximum(slot, 0), axis=1) + bias_ref[:, cols]
        codes_ref[:, cols] = jnp.where(slot >= 0, value, 0.0).astype(BF16)


def decode_other_kernel(packed_ref, slot_ref, bias_ref, w_ref, codes_ref, part_ref):
    spread_codes(1, packed_ref, slot_ref, bias_ref, codes_ref)
    y = jnp.dot(codes_ref[...], w_ref[...], preferred_element_type=F32)
    part_ref[...] = y.astype(BF16)


def decode_own_kernel(packed_ref, slot_ref, bias_ref, w_ref, codes_ref, part_ref):
    spread_codes(0, packed_ref, slot_ref, bias_ref, codes_ref)
    part_ref[...] = jnp.dot(codes_ref[...], w_ref[...], preferred_element_type=F32)


def encoder_grad_kernel(tok_ref, packed_ref, slot_ref, x_ref, out_ref, bias_ref, sum_ref, grad_ref):
    step = pl.program_id(0)

    @pl.when(step == 0)
    def _():
        sum_ref[...] = packed_sum(packed_ref)

    packed = sum_ref[...]
    rows = packed.shape[0]
    width = grad_ref.shape[1]
    totals = []
    for j in range(width // LANES):
        cols = pl.ds(j * LANES, LANES)
        total = jnp.zeros((1, LANES), F32)
        for m in range(2):
            slot = slot_ref[m, :, cols]
            value = jnp.take_along_axis(packed, jnp.maximum(slot, 0), axis=1)
            grad = jnp.where(slot >= 0, value, 0.0).astype(BF16)
            grad_ref[m * rows : (m + 1) * rows, cols] = grad
            total = total + jnp.sum(grad.astype(F32), axis=0, keepdims=True)
        totals.append(total)
    out_ref[...] = jnp.dot(
        x_ref[...], grad_ref[...], preferred_element_type=F32
    ).astype(BF16)
    kept = bias_ref.shape[1] // width
    for i in range(kept):

        @pl.when(step == tok_ref[0] * kept + i)
        def _():
            for j, total in enumerate(totals):
                bias_ref[:, i * width + j * LANES : i * width + (j + 1) * LANES] = total


def encoder_grad_call(tok, packed, slot, shifted_t, block=256):
    rows, latents = slot.shape[1:]
    width = shifted_t.shape[0]
    return pl.pallas_call(
        encoder_grad_kernel,
        grid=(latents // block,),
        in_specs=[
            pl.BlockSpec(memory_space=pltpu.SMEM),
            pl.BlockSpec(packed.shape, lambda i: (0, 0, 0)),
            pl.BlockSpec((2, rows, block), lambda i: (0, 0, i)),
            pl.BlockSpec(shifted_t.shape, lambda i: (0, 0)),
        ],
        out_specs=(
            pl.BlockSpec((width, block), lambda i: (0, i)),
            pl.BlockSpec((1, latents // 2), lambda i: (0, 0)),
        ),
        out_shape=(
            jax.ShapeDtypeStruct((width, latents), BF16),
            jax.ShapeDtypeStruct((1, latents // 2), F32),
        ),
        scratch_shapes=[pltpu.VMEM(packed.shape[1:], F32), pltpu.VMEM((2 * rows, block), BF16)],
        compiler_params=PARAMS,
    )(tok, packed, slot, shifted_t)


def swap_cores(x):
    return lax.ppermute(x, "core", [(0, 1), (1, 0)])


def exchange(x, axes):
    return lax.all_to_all(x, axes, 0, 0)


FEATURES = ("section", "tok")
COLUMN = ("yh", "z")


def body(
    residual, center, whiten, decoder_bias, encoder_weight, encoder_bias, decoder_weight, chosen
):
    core = lax.axis_index("core")
    tok = lax.axis_index("tok")
    width = encoder_weight.shape[0]
    latents = encoder_bias.shape[0]
    features = lax.axis_size(FEATURES)
    column = lax.axis_size(COLUMN)
    first = ((lax.axis_index("yh") * 8 + lax.axis_index("z")) * 2 + core) * latents

    own_picks = lax.dynamic_index_in_dim(chosen, core, 0, keepdims=False)
    other_picks = lax.dynamic_index_in_dim(chosen, 1 - core, 0, keepdims=False)
    place = jnp.concatenate([own_picks, other_picks], axis=1).astype(jnp.int32) - first
    rows = place.shape[0]

    out = jnp.broadcast_to(residual, (features,) + residual.shape[1:])
    arrived = exchange(out, ("tok", "section")).reshape(2, rows, -1)
    own_rows = lax.dynamic_index_in_dim(arrived, core, 0, keepdims=False)
    other_rows = lax.dynamic_index_in_dim(arrived, 1 - core, 0, keepdims=False)
    whiten_cols = lax.dynamic_slice_in_dim(whiten, tok * width, width, 1)
    bias_cols = lax.dynamic_slice_in_dim(decoder_bias, tok * width, width, 0)[None]

    rows_bf16 = jax.ShapeDtypeStruct((rows, width), BF16)
    center = center[None]
    white_flops = 2 * rows * width * center.shape[1]
    other_part = call(
        whiten_other_kernel, rows_bf16, (other_rows, center, whiten_cols), white_flops, 2**21
    )
    from_core = swap_cores(other_part)
    own_part = call(
        whiten_own_kernel, rows_bf16, (own_rows, center, whiten_cols, from_core), white_flops, 2**21
    )
    own_part, place_later = lax.optimization_barrier((own_part, place))
    slot = call(
        find_kernel,
        jax.ShapeDtypeStruct((2, rows, latents), jnp.int32),
        (place_later,),
        flops=2 * 64 * 2 * rows * latents,
        moved=8 * rows * latents,
    )
    shares = (column, rows // column, width)
    parts = exchange(own_part.reshape(shares), COLUMN)
    parts, slot = lax.optimization_barrier((parts, slot))
    share_bf16 = jax.ShapeDtypeStruct(shares[1:], BF16)
    shares_bf16 = jax.ShapeDtypeStruct(shares, BF16)
    whitened, out = call(
        shift_kernel, (share_bf16, shares_bf16), (parts, bias_cols), 0, 2**20
    )
    own_shifted = exchange(out, COLUMN).reshape(rows, width)
    other_shifted = swap_cores(own_shifted)

    flops = 2 * rows * width * latents
    moved = 2 * width * latents + 4 * rows * width
    packed_f32 = jax.ShapeDtypeStruct((rows, LANES), F32)
    packed_all = jax.ShapeDtypeStruct((features, rows, LANES), BF16)

    def packed_product(contract, own, other, weight):
        mine = call(
            functools.partial(product_pick_kernel, contract),
            packed_f32,
            (own, weight, place),
            flops,
            moved,
        )
        both = call(
            functools.partial(product_join_kernel, contract),
            packed_all,
            (other, weight, place, mine),
            flops,
            moved,
        )
        return exchange(both, FEATURES)

    encoded = packed_product(0, own_shifted, other_shifted, encoder_weight)

    codes_bf16 = jax.ShapeDtypeStruct((rows, latents), BF16)
    bias_row = encoder_bias[None]
    other_codes, other_part = call(
        decode_other_kernel,
        (codes_bf16, rows_bf16),
        (encoded, slot, bias_row, decoder_weight),
        flops,
        moved,
    )
    from_core = swap_cores(other_part)
    own_codes, own_part = call(
        decode_own_kernel,
        (codes_bf16, jax.ShapeDtypeStruct((rows, width), F32)),
        (encoded, slot, bias_row, decoder_weight),
        flops,
        moved,
    )
    parts = (own_part + from_core.astype(F32)).astype(BF16)
    parts = exchange(parts.reshape(shares), COLUMN)
    out = call(error_kernel, shares_bf16, (parts, bias_cols, whitened), 0, 2**20)
    own_grad = exchange(out, COLUMN).reshape(rows, width)
    other_grad = swap_cores(own_grad)

    code_grad = packed_product(1, own_grad, other_grad, decoder_weight)

    codes = jnp.concatenate([own_codes, other_codes], axis=0)
    out_grad = jnp.concatenate([own_grad, other_grad], axis=0)
    decoder_grad = lax.dot_general(
        codes, out_grad, (((0,), (0,)), ((), ())), preferred_element_type=F32
    ).astype(BF16)

    shifted_t = jnp.concatenate([own_shifted, other_shifted], axis=0).T
    encoder_grad, bias_grad = encoder_grad_call(
        tok.astype(jnp.int32)[None], code_grad, slot, shifted_t
    )
    return encoder_grad, decoder_grad, bias_grad[0]


def solution(mesh):
    fine = Mesh(mesh.devices.reshape(4, 2, 8, 2, 2), ("section", "yh", "z", "core", "tok"))
    lat = ("yh", "z", "core")
    return jax.shard_map(
        body,
        mesh=fine,
        in_specs=(
            P("tok", "section", lat),
            P(lat),
            P(lat, "section"),
            P("section"),
            P(("section", "tok"), lat),
            P(lat),
            P(lat, ("section", "tok")),
            P(),
        ),
        out_specs=(P(("section", "tok"), lat), P(lat, ("section", "tok")), P(lat + ("tok",))),
        check_vma=False,
    )
```

```python
import functools

import jax
import jax.numpy as jnp
from jax import lax
from jax.experimental import pallas as pl
from jax.experimental.pallas import tpu as pltpu
from jax.sharding import Mesh
from jax.sharding import PartitionSpec as P

grad_scale = 0.125
LANES = 128
F32 = jnp.float32
BF16 = jnp.bfloat16
HERE = pl.BlockSpec(memory_space=pltpu.VMEM)
SCALARS = pl.BlockSpec(memory_space=pltpu.SMEM)
ANY = pl.BlockSpec(memory_space=pl.ANY)
HBM = pl.BlockSpec(memory_space=pltpu.HBM)
MIB = 1024 * 1024
SMALL, MIDDLE, MOST = 12, 24, 62
COPIES = pltpu.SemaphoreType.DMA
ROW_BLOCKS = 4
FEATURES = ("section", "tok")
COLUMN = ("yh", "z")
CORE, TOK, FIRST, FIRST2 = range(4)


def spec(*shape, dtype=BF16):
    return jax.ShapeDtypeStruct(shape, dtype)


def call(kernel, ins, outs, operands, scratch=(), flops=0, moved=2**20, vmem=60):
    return pl.pallas_call(
        kernel,
        in_specs=list(ins),
        out_specs=tuple(place for place, _ in outs),
        out_shape=tuple(shape for _, shape in outs),
        scratch_shapes=list(scratch),
        compiler_params=pltpu.CompilerParams(vmem_limit_bytes=vmem * MIB),
        cost_estimate=pl.CostEstimate(flops=flops, bytes_accessed=moved, transcendentals=0),
    )(*operands)


def start(source, target, sem):
    copy = pltpu.make_async_copy(source, target, sem)
    copy.start()
    return copy


def place_kernel(latents, at_ref, chosen_ref, packed_ref, wide_ref):
    picked = chosen_ref[at_ref[CORE]]
    own, other = picked - at_ref[FIRST], picked - at_ref[FIRST2]
    wide_ref[...] = jnp.concatenate([own, other], axis=1)
    place = jnp.where((other >= 0) & (other < latents), other + latents, -1)
    place = jnp.where((own >= 0) & (own < latents), own, place)
    half = place.shape[0] // 2
    packed_ref[...] = jnp.concatenate([place[:half], place[half:]], axis=1)


def find_kernel(wide_ref, slot_ref, slot2_ref, found):
    rows, width = slot_ref.shape
    half, picks = rows // 2, LANES // 2
    column = lax.broadcasted_iota(jnp.int32, (8, width), 1)

    def step(i, carry):
        own = pl.ds(pl.multiple_of(i * 8, 8), 8)
        place = wide_ref[own, :]
        for n in range(2):
            slot = jnp.full((8, width), -1, jnp.int32)
            for k in range(picks):
                at = n * picks + k
                slot = jnp.where(place[:, at : at + 1] == column, k, slot)
            found[n, own, :] = slot
        return carry

    def pack(i, carry):
        own = pl.ds(pl.multiple_of(i * 16, 16), 16)
        lane = jnp.where(i * 16 >= half, picks, 0)
        for n, out in enumerate((slot_ref, slot2_ref)):
            slot = found[n, own, :]
            out[own, :] = jnp.where(slot >= 0, slot + lane, slot).astype(F32).astype(BF16)
        return carry

    lax.fori_loop(0, rows // 8, step, 0)
    lax.fori_loop(0, rows // 16, pack, 0)


def pick(low, high, place, chunk, j, y):
    half = place.shape[0]
    here = chunk == j
    low = jnp.where(here, jnp.take_along_axis(y[:half], place, axis=1), low)
    high = jnp.where(here, jnp.take_along_axis(y[half:], place, axis=1), high)
    return low, high


def spread(packed, slot, cols):
    lane = slot[:, cols].astype(F32).astype(jnp.int32)
    half = packed.shape[0]
    value = jnp.concatenate(
        [
            jnp.take_along_axis(packed, jnp.maximum(lane[:half], 0), axis=1),
            jnp.take_along_axis(packed, jnp.maximum(lane[half:], 0), axis=1),
        ],
        axis=0,
    )
    return value, lane >= 0


def sum_of(parts_ref):
    total = parts_ref[0].astype(F32)
    for i in range(1, parts_ref.shape[0]):
        total = total + parts_ref[i].astype(F32)
    return total


def whiten_other_kernel(x_ref, w_ref, out_ref):
    out_ref[...] = jnp.dot(x_ref[...], w_ref[...], preferred_element_type=F32).astype(BF16)


def whiten_own_kernel(x_ref, w_ref, add_ref, out_ref, ready, sems):
    y = jnp.dot(x_ref[...], w_ref[...], preferred_element_type=F32) + add_ref[...].astype(F32)
    ready[...] = y.astype(BF16)
    start(ready, out_ref, sems.at[0]).wait()


def own_bias(at_ref, bias_ref, width):
    return bias_ref[:, pl.ds(pl.multiple_of(at_ref[TOK] * width, width), width)]


def shift_kernel(at_ref, parts_ref, bias_ref, white_ref, out_ref):
    white = sum_of(parts_ref).astype(BF16)
    white_ref[...] = white
    shifted = (white.astype(F32) - own_bias(at_ref, bias_ref, white.shape[1])).astype(BF16)
    for i in range(out_ref.shape[0]):
        out_ref[i] = shifted


def error_kernel(at_ref, parts_ref, bias_ref, white_ref, out_ref):
    rebuilt = sum_of(parts_ref) + own_bias(at_ref, bias_ref, white_ref.shape[1])
    grad = (grad_scale * (rebuilt - white_ref[...].astype(F32))).astype(BF16)
    for i in range(out_ref.shape[0]):
        out_ref[i] = grad


def product_kernel(contract, x_ref, place_ref, w_ref, w2_ref, out_ref, held, sems):
    copies = [start(w_ref, held.at[0], sems.at[0]), start(w2_ref, held.at[1], sems.at[1])]
    place = place_ref[...]
    lane, chunk = place & (LANES - 1), place >> 7
    low = high = jnp.zeros(place.shape, F32)
    for n in range(2):
        copies[n].wait()
        y = lax.dot_general(
            x_ref[...], held[n], (((1,), (contract,)), ((), ())), preferred_element_type=F32
        )
        blocks = y.shape[1] // LANES
        for j in range(blocks):
            part = y[:, j * LANES : (j + 1) * LANES]
            low, high = pick(low, high, lane, chunk, n * blocks + j, part)
    column = lax.broadcasted_iota(jnp.int32, place.shape, 1)
    packed = jnp.where(column < LANES // 2, low, high).astype(BF16)
    for i in range(out_ref.shape[0]):
        out_ref[i] = packed


def spread_codes(packed, slot, bias_ref, codes_ref):
    for j in range(codes_ref.shape[1] // LANES):
        cols = pl.ds(j * LANES, LANES)
        value, there = spread(packed, slot, cols)
        codes_ref[:, cols] = jnp.where(there, value + bias_ref[:, cols], 0.0).astype(BF16)


def decode_kernel(
    parts_ref,
    slot_ref,
    slot2_ref,
    bias_ref,
    bias2_ref,
    w_ref,
    w2_ref,
    packed_ref,
    out_ref,
    codes,
    slots,
    held,
    sems,
):
    found = [start(slot_ref, slots.at[0], sems.at[2]), start(slot2_ref, slots.at[1], sems.at[3])]
    copies = [start(w_ref, held.at[0], sems.at[0]), start(w2_ref, held.at[1], sems.at[1])]
    packed = sum_of(parts_ref)
    packed_ref[...] = packed
    for n, bias in enumerate((bias_ref, bias2_ref)):
        found[n].wait()
        spread_codes(packed, slots.at[n], bias, codes.at[n])
    for copy in copies:
        copy.wait()
    y = jnp.dot(codes[0], held[0], preferred_element_type=F32)
    y = y + jnp.dot(codes[1], held[1], preferred_element_type=F32)
    out_ref[...] = y.astype(BF16)


ROWS_BY_ROWS = (((0,), (0,)), ((), ()))


def codes_kernel(packed_ref, packed2_ref, slot_ref, slot2_ref, bias_ref, out_ref, out2_ref):
    spread_codes(packed_ref[...], slot_ref, bias_ref, out_ref)
    spread_codes(packed2_ref[...], slot2_ref, bias_ref, out2_ref)


def decoder_grad_kernel(codes_ref, codes2_ref, grad_ref, grad2_ref, out_ref):
    y = lax.dot_general(codes_ref[...], grad_ref[...], ROWS_BY_ROWS, preferred_element_type=F32)
    y = y + lax.dot_general(
        codes2_ref[...], grad2_ref[...], ROWS_BY_ROWS, preferred_element_type=F32
    )
    out_ref[...] = y.astype(BF16)


def spread_grad(parts_ref, slot_ref, grad):
    packed = sum_of(parts_ref)
    for j in range(grad.shape[1] // LANES):
        cols = pl.ds(j * LANES, LANES)
        value, there = spread(packed, slot_ref, cols)
        grad[:, cols] = jnp.where(there, value, 0.0).astype(BF16)


def row_sum(at_ref, grad, kept):
    ones = jnp.ones((16, grad.shape[0]), BF16)
    cols = pl.ds(pl.multiple_of(at_ref[TOK] * kept, kept), kept)
    return jnp.dot(ones, grad[:, cols], preferred_element_type=F32)[:1]


def first_grad_kernel(at_ref, parts_ref, slot_ref, x_ref, out_ref, bias_ref, grad):
    spread_grad(parts_ref, slot_ref, grad)
    bias_ref[...] = row_sum(at_ref, grad, bias_ref.shape[1])
    out_ref[...] = lax.dot_general(
        x_ref[...], grad[...], ROWS_BY_ROWS, preferred_element_type=F32
    )


def second_grad_kernel(
    at_ref, parts_ref, slot_ref, x_ref, first_ref, first_bias_ref, out_ref, bias_ref, grad, made, sems
):
    spread_grad(parts_ref, slot_ref, grad)
    bias_ref[...] = first_bias_ref[...] + row_sum(at_ref, grad, bias_ref.shape[1])
    height = made.shape[0] // ROW_BLOCKS
    copies = []
    for b in range(ROW_BLOCKS):
        own = pl.ds(b * height, height)
        y = lax.dot_general(x_ref[:, own], grad[...], ROWS_BY_ROWS, preferred_element_type=F32)
        made[own, :] = (y + first_ref[own, :]).astype(BF16)
        copies.append(start(made.at[own], out_ref.at[own], sems.at[b]))
    for copy in copies:
        copy.wait()


def swap(x):
    return lax.ppermute(x, "core", [(0, 1), (1, 0)])


def exchange(x, axes):
    return lax.all_to_all(x, axes, 0, 0)


def body(
    residual, center, whiten, decoder_bias, encoder_weight, encoder_bias, decoder_weight, chosen
):
    core = lax.axis_index("core")
    width = encoder_weight.shape[0]
    latents = encoder_bias.shape[0]
    rows, picks = chosen.shape[1:]
    inputs = center.shape[0]
    receivers = lax.axis_size(FEATURES)
    column = lax.axis_size(COLUMN)
    chip = (lax.axis_index("yh") * lax.axis_size("z") + lax.axis_index("z")) * 2
    at = jnp.stack(
        [core, lax.axis_index("tok"), (chip + core) * latents, (chip + 1 - core) * latents]
    ).astype(jnp.int32)

    centered = (residual[0].astype(F32) - center).astype(BF16)
    out = jnp.broadcast_to(centered[None], (receivers,) + centered.shape)
    arrived = exchange(out, ("tok", "section")).reshape(2, rows, inputs)
    own_rows = lax.dynamic_index_in_dim(arrived, core, 0, keepdims=False)
    other_rows = lax.dynamic_index_in_dim(arrived, 1 - core, 0, keepdims=False)
    whiten_cols = lax.dynamic_slice_in_dim(whiten, at[TOK] * width, width, 1)
    flops = 2 * rows * width * inputs
    (part,) = call(
        whiten_other_kernel,
        (HERE, HERE),
        [(HERE, spec(rows, width))],
        (other_rows, whiten_cols),
        (),
        flops,
        vmem=SMALL,
    )
    (part,) = call(
        whiten_own_kernel,
        (HERE, HERE, HERE),
        [(HBM, spec(rows, width))],
        (own_rows, whiten_cols, swap(part)),
        [pltpu.VMEM((rows, width), BF16), COPIES((1,))],
        flops,
        vmem=SMALL,
    )
    shares = (column, rows // column, width)
    share, all_shares = spec(*shares[1:]), spec(*shares)
    bias_row, decoder_bias = encoder_bias[None], decoder_bias[None]

    part, listed, encoder_weight, decoder_weight, bias_row = lax.optimization_barrier(
        (part, chosen, encoder_weight, decoder_weight, bias_row)
    )
    place, wide = call(
        functools.partial(place_kernel, latents),
        (SCALARS, HERE),
        [
            (HERE, spec(rows // 2, LANES, dtype=jnp.int32)),
            (HERE, spec(rows, LANES, dtype=jnp.int32)),
        ],
        (at, listed),
        vmem=SMALL,
    )
    slot, slot2 = call(
        find_kernel,
        (HERE,),
        [(HERE, spec(rows, latents)), (HERE, spec(rows, latents))],
        (wide,),
        [pltpu.VMEM((2, rows, latents), jnp.int32)],
        4 * picks * rows * latents,
    )
    encoder_weight2, decoder_weight2 = swap(encoder_weight), swap(decoder_weight)
    bias_row2 = swap(bias_row)
    parts, slot, slot2, place, encoder_weight2, decoder_weight2, bias_row2 = lax.optimization_barrier(
        (
            exchange(part.reshape(shares), COLUMN),
            slot,
            slot2,
            place,
            encoder_weight2,
            decoder_weight2,
            bias_row2,
        )
    )
    whitened, out = call(
        shift_kernel,
        (SCALARS, HERE, HERE),
        [(HERE, share), (HERE, all_shares)],
        (at, parts, decoder_bias),
        vmem=SMALL,
    )
    shifted = exchange(out, COLUMN).reshape(rows, width)

    flops = 4 * rows * width * latents
    moved = 4 * width * latents
    weights_held = [pltpu.VMEM((2, width, latents), BF16), COPIES((2,))]

    def chosen_product(contract, x, weight, weight2):
        (packed,) = call(
            functools.partial(product_kernel, contract),
            (HERE, HERE, ANY, ANY),
            [(HERE, spec(receivers, rows // 2, LANES))],
            (x, place, weight, weight2),
            weights_held,
            flops,
            moved,
            MOST,
        )
        return packed

    encoded = chosen_product(0, shifted, encoder_weight, encoder_weight2)
    encoded, shifted = lax.optimization_barrier((encoded, shifted))
    shifted2, other_slot = swap(shifted), swap(slot2)
    encoded = exchange(encoded, FEATURES)
    packed, part = call(
        decode_kernel,
        (HERE, ANY, ANY, HERE, HERE, ANY, ANY),
        [(HERE, spec(rows // 2, LANES, dtype=F32)), (HERE, spec(rows, width))],
        (encoded, slot, slot2, bias_row, bias_row2, decoder_weight, decoder_weight2),
        [
            pltpu.VMEM((2, rows, latents), BF16),
            pltpu.VMEM((2, rows, latents), BF16),
            pltpu.VMEM((2, width, latents), BF16),
            COPIES((4,)),
        ],
        flops,
        moved,
        MOST,
    )
    part, packed = lax.optimization_barrier((part, packed))
    codes, codes2 = call(
        codes_kernel,
        (HERE,) * 5,
        [(HERE, spec(rows, latents)), (HERE, spec(rows, latents))],
        (packed, swap(packed), slot, other_slot, bias_row),
    )
    parts, codes, codes2, shifted2, other_slot = lax.optimization_barrier(
        (exchange(part.reshape(shares), COLUMN), codes, codes2, shifted2, other_slot)
    )
    (out,) = call(
        error_kernel,
        (SCALARS, HERE, HERE, HERE),
        [(HERE, all_shares)],
        (at, parts, decoder_bias, whitened),
        vmem=SMALL,
    )
    grad = exchange(out, COLUMN).reshape(rows, width)

    packed = chosen_product(1, grad, decoder_weight, decoder_weight2)
    packed, grad = lax.optimization_barrier((packed, grad))
    (decoder_grad,) = call(
        decoder_grad_kernel,
        (HERE,) * 4,
        [(HERE, spec(latents, width))],
        (codes, codes2, grad, swap(grad)),
        (),
        flops,
        moved,
    )
    code_grad, decoder_grad = lax.optimization_barrier(
        (exchange(packed, FEATURES), decoder_grad)
    )
    code_grad2 = swap(code_grad)
    bias_half = spec(1, latents // 2, dtype=F32)
    first_grad, first_bias = call(
        first_grad_kernel,
        (SCALARS, HERE, HERE, HERE),
        [(HERE, spec(width, latents, dtype=F32)), (HERE, bias_half)],
        (at, code_grad, slot, shifted),
        [pltpu.VMEM((rows, latents), BF16)],
        flops,
        moved,
        MIDDLE,
    )
    encoder_grad, bias_grad = call(
        second_grad_kernel,
        (SCALARS, HERE, HERE, HERE, HERE, HERE),
        [(ANY, spec(width, latents)), (HERE, bias_half)],
        (at, code_grad2, other_slot, shifted2, first_grad, first_bias),
        [
            pltpu.VMEM((rows, latents), BF16),
            pltpu.VMEM((width, latents), BF16),
            COPIES((ROW_BLOCKS,)),
        ],
        flops,
        moved,
        MIDDLE,
    )
    return encoder_grad, decoder_grad, bias_grad[0]


def solution(mesh):
    fine = Mesh(mesh.devices.reshape(4, 2, 8, 2, 2), ("section", "yh", "z", "core", "tok"))
    lat = ("yh", "z", "core")
    return jax.shard_map(
        body,
        mesh=fine,
        in_specs=(
            P("tok", "section", lat),
            P(lat),
            P(lat, "section"),
            P("section"),
            P(("section", "tok"), lat),
            P(lat),
            P(lat, ("section", "tok")),
            P(),
        ),
        out_specs=(P(("section", "tok"), lat), P(lat, ("section", "tok")), P(lat + ("tok",))),
        check_vma=False,
    )
```

```python
import functools

import jax
import jax.numpy as jnp
from jax import lax
from jax.experimental import pallas as pl
from jax.experimental.pallas import tpu as pltpu
from jax.sharding import Mesh
from jax.sharding import PartitionSpec as P

grad_scale = 0.125
LANES = 128
F32 = jnp.float32
BF16 = jnp.bfloat16
HERE = pl.BlockSpec(memory_space=pltpu.VMEM)
SCALARS = pl.BlockSpec(memory_space=pltpu.SMEM)
ANY = pl.BlockSpec(memory_space=pl.ANY)
HBM = pl.BlockSpec(memory_space=pltpu.HBM)
MIB = 1024 * 1024
SMALL, MIDDLE, MOST = 12, 24, 24
COPIES = pltpu.SemaphoreType.DMA
ROW_BLOCKS = 4
FEATURES = ("section", "tok")
COLUMN = ("yh", "z")
CORE, TOK, FIRST, FIRST2 = range(4)


def spec(*shape, dtype=BF16):
    return jax.ShapeDtypeStruct(shape, dtype)


def call(kernel, ins, outs, operands, scratch=(), flops=0, moved=2**20, vmem=60):
    return pl.pallas_call(
        kernel,
        in_specs=list(ins),
        out_specs=tuple(place for place, _ in outs),
        out_shape=tuple(shape for _, shape in outs),
        scratch_shapes=list(scratch),
        compiler_params=pltpu.CompilerParams(vmem_limit_bytes=vmem * MIB),
        cost_estimate=pl.CostEstimate(flops=flops, bytes_accessed=moved, transcendentals=0),
    )(*operands)


def start(source, target, sem):
    copy = pltpu.make_async_copy(source, target, sem)
    copy.start()
    return copy


def place_kernel(latents, at_ref, chosen_ref, packed_ref, wide_ref):
    picked = chosen_ref[at_ref[CORE]]
    own, other = picked - at_ref[FIRST], picked - at_ref[FIRST2]
    wide_ref[...] = jnp.concatenate([own, other], axis=1)
    place = jnp.where((other >= 0) & (other < latents), other + latents, -1)
    place = jnp.where((own >= 0) & (own < latents), own, place)
    half = place.shape[0] // 2
    packed_ref[...] = jnp.concatenate([place[:half], place[half:]], axis=1)


def find_kernel(wide_ref, slot_ref, slot2_ref, found):
    rows, width = slot_ref.shape
    half, picks = rows // 2, LANES // 2
    column = lax.broadcasted_iota(jnp.int32, (8, width), 1)

    def step(i, carry):
        own = pl.ds(pl.multiple_of(i * 8, 8), 8)
        place = wide_ref[own, :]
        for n in range(2):
            slot = jnp.full((8, width), -1, jnp.int32)
            for k in range(picks):
                at = n * picks + k
                slot = jnp.where(place[:, at : at + 1] == column, k, slot)
            found[n, own, :] = slot
        return carry

    def pack(i, carry):
        own = pl.ds(pl.multiple_of(i * 16, 16), 16)
        lane = jnp.where(i * 16 >= half, picks, 0)
        for n, out in enumerate((slot_ref, slot2_ref)):
            slot = found[n, own, :]
            out[own, :] = jnp.where(slot >= 0, slot + lane, slot).astype(F32).astype(BF16)
        return carry

    lax.fori_loop(0, rows // 8, step, 0)
    lax.fori_loop(0, rows // 16, pack, 0)


def pick(low, high, place, chunk, j, y):
    half = place.shape[0]
    here = chunk == j
    low = jnp.where(here, jnp.take_along_axis(y[:half], place, axis=1), low)
    high = jnp.where(here, jnp.take_along_axis(y[half:], place, axis=1), high)
    return low, high


def spread(packed, slot, cols):
    lane = slot[:, cols].astype(F32).astype(jnp.int32)
    half = packed.shape[0]
    value = jnp.concatenate(
        [
            jnp.take_along_axis(packed, jnp.maximum(lane[:half], 0), axis=1),
            jnp.take_along_axis(packed, jnp.maximum(lane[half:], 0), axis=1),
        ],
        axis=0,
    )
    return value, lane >= 0


def sum_of(parts_ref):
    total = parts_ref[0].astype(F32)
    for i in range(1, parts_ref.shape[0]):
        total = total + parts_ref[i].astype(F32)
    return total


def whiten_other_kernel(x_ref, w_ref, out_ref):
    out_ref[...] = jnp.dot(x_ref[...], w_ref[...], preferred_element_type=F32).astype(BF16)


def whiten_own_kernel(x_ref, w_ref, add_ref, out_ref, ready, sems):
    y = jnp.dot(x_ref[...], w_ref[...], preferred_element_type=F32) + add_ref[...].astype(F32)
    ready[...] = y.astype(BF16)
    start(ready, out_ref, sems.at[0]).wait()


def own_bias(at_ref, bias_ref, width):
    return bias_ref[:, pl.ds(pl.multiple_of(at_ref[TOK] * width, width), width)]


def shift_kernel(at_ref, parts_ref, bias_ref, white_ref, out_ref):
    white = sum_of(parts_ref).astype(BF16)
    white_ref[...] = white
    shifted = (white.astype(F32) - own_bias(at_ref, bias_ref, white.shape[1])).astype(BF16)
    for i in range(out_ref.shape[0]):
        out_ref[i] = shifted


def error_kernel(at_ref, parts_ref, bias_ref, white_ref, out_ref):
    rebuilt = sum_of(parts_ref) + own_bias(at_ref, bias_ref, white_ref.shape[1])
    grad = (grad_scale * (rebuilt - white_ref[...].astype(F32))).astype(BF16)
    for i in range(out_ref.shape[0]):
        out_ref[i] = grad


def product_kernel(contract, x_ref, place_ref, w_ref, w2_ref, out_ref, held, sems):
    copy = start(w_ref, held, sems.at[0])
    place = place_ref[...]
    lane, chunk = place & (LANES - 1), place >> 7
    low = high = jnp.zeros(place.shape, F32)
    for n, weight in ((1, w2_ref), (0, held)):
        if n == 0:
            copy.wait()
        y = lax.dot_general(
            x_ref[...], weight[...], (((1,), (contract,)), ((), ())), preferred_element_type=F32
        )
        blocks = y.shape[1] // LANES
        for j in range(blocks):
            part = y[:, j * LANES : (j + 1) * LANES]
            low, high = pick(low, high, lane, chunk, n * blocks + j, part)
    column = lax.broadcasted_iota(jnp.int32, place.shape, 1)
    packed = jnp.where(column < LANES // 2, low, high).astype(BF16)
    for i in range(out_ref.shape[0]):
        out_ref[i] = packed


def spread_codes(packed, slot, bias_ref, codes_ref):
    for j in range(codes_ref.shape[1] // LANES):
        cols = pl.ds(j * LANES, LANES)
        value, there = spread(packed, slot, cols)
        codes_ref[:, cols] = jnp.where(there, value + bias_ref[:, cols], 0.0).astype(BF16)


def decode_kernel(
    parts_ref,
    slot_ref,
    slot2_ref,
    bias_ref,
    bias2_ref,
    w_ref,
    w2_ref,
    packed_ref,
    out_ref,
    codes,
    slots,
    held,
    sems,
):
    found = [start(slot_ref, slots.at[0], sems.at[1]), start(slot2_ref, slots.at[1], sems.at[2])]
    copy = start(w_ref, held, sems.at[0])
    packed = sum_of(parts_ref)
    packed_ref[...] = packed
    for n, bias in enumerate((bias_ref, bias2_ref)):
        found[n].wait()
        spread_codes(packed, slots.at[n], bias, codes.at[n])
    y = jnp.dot(codes[1], w2_ref[...], preferred_element_type=F32)
    copy.wait()
    y = y + jnp.dot(codes[0], held[...], preferred_element_type=F32)
    out_ref[...] = y.astype(BF16)


ROWS_BY_ROWS = (((0,), (0,)), ((), ()))


def codes_kernel(packed_ref, packed2_ref, slot_ref, slot2_ref, bias_ref, out_ref, out2_ref):
    spread_codes(packed_ref[...], slot_ref, bias_ref, out_ref)
    spread_codes(packed2_ref[...], slot2_ref, bias_ref, out2_ref)


def decoder_grad_kernel(codes_ref, codes2_ref, grad_ref, grad2_ref, out_ref):
    y = lax.dot_general(codes_ref[...], grad_ref[...], ROWS_BY_ROWS, preferred_element_type=F32)
    y = y + lax.dot_general(
        codes2_ref[...], grad2_ref[...], ROWS_BY_ROWS, preferred_element_type=F32
    )
    out_ref[...] = y.astype(BF16)


def spread_grad(parts_ref, slot_ref, grad):
    packed = sum_of(parts_ref)
    for j in range(grad.shape[1] // LANES):
        cols = pl.ds(j * LANES, LANES)
        value, there = spread(packed, slot_ref, cols)
        grad[:, cols] = jnp.where(there, value, 0.0).astype(BF16)


def row_sum(at_ref, grad, kept):
    ones = jnp.ones((16, grad.shape[0]), BF16)
    cols = pl.ds(pl.multiple_of(at_ref[TOK] * kept, kept), kept)
    return jnp.dot(ones, grad[:, cols], preferred_element_type=F32)[:1]


def first_grad_kernel(at_ref, parts_ref, slot_ref, x_ref, out_ref, bias_ref, grad):
    spread_grad(parts_ref, slot_ref, grad)
    bias_ref[...] = row_sum(at_ref, grad, bias_ref.shape[1])
    out_ref[...] = lax.dot_general(
        x_ref[...], grad[...], ROWS_BY_ROWS, preferred_element_type=F32
    )


def second_grad_kernel(
    at_ref, parts_ref, slot_ref, x_ref, first_ref, first_bias_ref, out_ref, bias_ref, grad, made, sems
):
    spread_grad(parts_ref, slot_ref, grad)
    bias_ref[...] = first_bias_ref[...] + row_sum(at_ref, grad, bias_ref.shape[1])
    height = made.shape[0] // ROW_BLOCKS
    copies = []
    for b in range(ROW_BLOCKS):
        own = pl.ds(b * height, height)
        y = lax.dot_general(x_ref[:, own], grad[...], ROWS_BY_ROWS, preferred_element_type=F32)
        made[own, :] = (y + first_ref[own, :]).astype(BF16)
        copies.append(start(made.at[own], out_ref.at[own], sems.at[b]))
    for copy in copies:
        copy.wait()


def swap(x):
    return lax.ppermute(x, "core", [(0, 1), (1, 0)])


def exchange(x, axes):
    return lax.all_to_all(x, axes, 0, 0)


def body(
    residual, center, whiten, decoder_bias, encoder_weight, encoder_bias, decoder_weight, chosen
):
    core = lax.axis_index("core")
    width = encoder_weight.shape[0]
    latents = encoder_bias.shape[0]
    rows, picks = chosen.shape[1:]
    inputs = center.shape[0]
    receivers = lax.axis_size(FEATURES)
    column = lax.axis_size(COLUMN)
    chip = (lax.axis_index("yh") * lax.axis_size("z") + lax.axis_index("z")) * 2
    at = jnp.stack(
        [core, lax.axis_index("tok"), (chip + core) * latents, (chip + 1 - core) * latents]
    ).astype(jnp.int32)

    centered = (residual[0].astype(F32) - center).astype(BF16)
    out = jnp.broadcast_to(centered[None], (receivers,) + centered.shape)
    out, listed = lax.optimization_barrier((out, chosen))
    place, wide = call(
        functools.partial(place_kernel, latents),
        (SCALARS, HERE),
        [
            (HERE, spec(rows // 2, LANES, dtype=jnp.int32)),
            (HERE, spec(rows, LANES, dtype=jnp.int32)),
        ],
        (at, listed),
        vmem=SMALL,
    )
    arrived, wide, place = lax.optimization_barrier(
        (exchange(out, ("tok", "section")), wide, place)
    )
    arrived = arrived.reshape(2, rows, inputs)
    own_rows = lax.dynamic_index_in_dim(arrived, core, 0, keepdims=False)
    other_rows = lax.dynamic_index_in_dim(arrived, 1 - core, 0, keepdims=False)
    whiten_cols = lax.dynamic_slice_in_dim(whiten, at[TOK] * width, width, 1)
    flops = 2 * rows * width * inputs
    (part,) = call(
        whiten_other_kernel,
        (HERE, HERE),
        [(HERE, spec(rows, width))],
        (other_rows, whiten_cols),
        (),
        flops,
        vmem=SMALL,
    )
    (part,) = call(
        whiten_own_kernel,
        (HERE, HERE, HERE),
        [(HBM, spec(rows, width))],
        (own_rows, whiten_cols, swap(part)),
        [pltpu.VMEM((rows, width), BF16), COPIES((1,))],
        flops,
        vmem=SMALL,
    )
    shares = (column, rows // column, width)
    share, all_shares = spec(*shares[1:]), spec(*shares)
    bias_row, decoder_bias = encoder_bias[None], decoder_bias[None]

    part, wide, bias_row = lax.optimization_barrier((part, wide, bias_row))
    slot, slot2 = call(
        find_kernel,
        (HERE,),
        [(HERE, spec(rows, latents)), (HERE, spec(rows, latents))],
        (wide,),
        [pltpu.VMEM((2, rows, latents), jnp.int32)],
        4 * picks * rows * latents,
    )
    bias_row2 = swap(bias_row)
    parts, slot, slot2, bias_row2 = lax.optimization_barrier(
        (exchange(part.reshape(shares), COLUMN), slot, slot2, bias_row2)
    )
    whitened, out = call(
        shift_kernel,
        (SCALARS, HERE, HERE),
        [(HERE, share), (HERE, all_shares)],
        (at, parts, decoder_bias),
        vmem=SMALL,
    )
    out, encoder_weight = lax.optimization_barrier((out, encoder_weight))
    encoder_weight2 = swap(encoder_weight)
    shifted = exchange(out, COLUMN).reshape(rows, width)

    flops = 4 * rows * width * latents
    moved = 4 * width * latents
    weight_held = [pltpu.VMEM((width, latents), BF16), COPIES((1,))]

    def chosen_product(contract, x, weight, weight2):
        (packed,) = call(
            functools.partial(product_kernel, contract),
            (HERE, HERE, ANY, HERE),
            [(HERE, spec(receivers, rows // 2, LANES))],
            (x, place, weight, weight2),
            weight_held,
            flops,
            moved,
            MOST,
        )
        return packed

    encoded = chosen_product(0, shifted, encoder_weight, encoder_weight2)
    encoded, shifted, weight = lax.optimization_barrier((encoded, shifted, decoder_weight))
    weight2 = swap(weight)
    shifted2, other_slot = swap(shifted), swap(slot2)
    encoded = exchange(encoded, FEATURES)
    packed, part = call(
        decode_kernel,
        (HERE, ANY, ANY, HERE, HERE, ANY, HERE),
        [(HERE, spec(rows // 2, LANES, dtype=F32)), (HERE, spec(rows, width))],
        (encoded, slot, slot2, bias_row, bias_row2, weight, weight2),
        [
            pltpu.VMEM((2, rows, latents), BF16),
            pltpu.VMEM((2, rows, latents), BF16),
            pltpu.VMEM((latents, width), BF16),
            COPIES((3,)),
        ],
        flops,
        moved,
        MOST,
    )
    part, packed, decoder_weight = lax.optimization_barrier((part, packed, decoder_weight))
    decoder_weight2 = swap(decoder_weight)
    codes, codes2 = call(
        codes_kernel,
        (HERE,) * 5,
        [(HERE, spec(rows, latents)), (HERE, spec(rows, latents))],
        (packed, swap(packed), slot, other_slot, bias_row),
    )
    parts, codes, codes2, shifted2, other_slot = lax.optimization_barrier(
        (exchange(part.reshape(shares), COLUMN), codes, codes2, shifted2, other_slot)
    )
    (out,) = call(
        error_kernel,
        (SCALARS, HERE, HERE, HERE),
        [(HERE, all_shares)],
        (at, parts, decoder_bias, whitened),
        vmem=SMALL,
    )
    grad = exchange(out, COLUMN).reshape(rows, width)

    packed = chosen_product(1, grad, decoder_weight, decoder_weight2)
    packed, grad = lax.optimization_barrier((packed, grad))
    (decoder_grad,) = call(
        decoder_grad_kernel,
        (HERE,) * 4,
        [(HERE, spec(latents, width))],
        (codes, codes2, grad, swap(grad)),
        (),
        flops,
        moved,
    )
    code_grad, decoder_grad = lax.optimization_barrier(
        (exchange(packed, FEATURES), decoder_grad)
    )
    code_grad2 = swap(code_grad)
    bias_half = spec(1, latents // 2, dtype=F32)
    first_grad, first_bias = call(
        first_grad_kernel,
        (SCALARS, HERE, HERE, HERE),
        [(HERE, spec(width, latents, dtype=F32)), (HERE, bias_half)],
        (at, code_grad, slot, shifted),
        [pltpu.VMEM((rows, latents), BF16)],
        flops,
        moved,
        MIDDLE,
    )
    encoder_grad, bias_grad = call(
        second_grad_kernel,
        (SCALARS, HERE, HERE, HERE, HERE, HERE),
        [(ANY, spec(width, latents)), (HERE, bias_half)],
        (at, code_grad2, other_slot, shifted2, first_grad, first_bias),
        [
            pltpu.VMEM((rows, latents), BF16),
            pltpu.VMEM((width, latents), BF16),
            COPIES((ROW_BLOCKS,)),
        ],
        flops,
        moved,
        MIDDLE,
    )
    return encoder_grad, decoder_grad, bias_grad[0]


def solution(mesh):
    fine = Mesh(mesh.devices.reshape(4, 2, 8, 2, 2), ("section", "yh", "z", "core", "tok"))
    lat = ("yh", "z", "core")
    return jax.shard_map(
        body,
        mesh=fine,
        in_specs=(
            P("tok", "section", lat),
            P(lat),
            P(lat, "section"),
            P("section"),
            P(("section", "tok"), lat),
            P(lat),
            P(lat, ("section", "tok")),
            P(),
        ),
        out_specs=(P(("section", "tok"), lat), P(lat, ("section", "tok")), P(lat + ("tok",))),
        check_vma=False,
    )
```

```python
import functools

import jax
import jax.numpy as jnp
from jax import lax
from jax.experimental import pallas as pl
from jax.experimental.pallas import tpu as pltpu
from jax.sharding import Mesh
from jax.sharding import PartitionSpec as P

grad_scale = 0.125
LANES = 128
F32 = jnp.float32
BF16 = jnp.bfloat16
HERE = pl.BlockSpec(memory_space=pltpu.VMEM)
SCALARS = pl.BlockSpec(memory_space=pltpu.SMEM)
ANY = pl.BlockSpec(memory_space=pl.ANY)
HBM = pl.BlockSpec(memory_space=pltpu.HBM)
MIB = 1024 * 1024
SMALL, MIDDLE, MOST = 12, 24, 24
COPIES = pltpu.SemaphoreType.DMA
ROW_BLOCKS = 8
FEATURES = ("section", "tok")
COLUMN = ("yh", "z")
CORE, TOK, FIRST, FIRST2 = range(4)


def spec(*shape, dtype=BF16):
    return jax.ShapeDtypeStruct(shape, dtype)


def call(kernel, ins, outs, operands, scratch=(), flops=0, moved=2**20, vmem=60):
    return pl.pallas_call(
        kernel,
        in_specs=list(ins),
        out_specs=tuple(place for place, _ in outs),
        out_shape=tuple(shape for _, shape in outs),
        scratch_shapes=list(scratch),
        compiler_params=pltpu.CompilerParams(vmem_limit_bytes=vmem * MIB),
        cost_estimate=pl.CostEstimate(flops=flops, bytes_accessed=moved, transcendentals=0),
    )(*operands)


def start(source, target, sem):
    copy = pltpu.make_async_copy(source, target, sem)
    copy.start()
    return copy


def place_kernel(latents, at_ref, chosen_ref, packed_ref, wide_ref):
    picked = chosen_ref[at_ref[CORE]]
    own, other = picked - at_ref[FIRST], picked - at_ref[FIRST2]
    wide_ref[...] = jnp.concatenate([own, other], axis=1)
    place = jnp.where((other >= 0) & (other < latents), other + latents, -1)
    place = jnp.where((own >= 0) & (own < latents), own, place)
    half = place.shape[0] // 2
    packed_ref[...] = jnp.concatenate([place[:half], place[half:]], axis=1)


def find_kernel(wide_ref, slot_ref, slot2_ref, found):
    rows, width = slot_ref.shape
    half, picks = rows // 2, LANES // 2
    column = lax.broadcasted_iota(jnp.int32, (8, width), 1)

    def step(i, carry):
        own = pl.ds(pl.multiple_of(i * 8, 8), 8)
        place = wide_ref[own, :]
        for n in range(2):
            slot = jnp.full((8, width), -1, jnp.int32)
            for k in range(picks):
                at = n * picks + k
                slot = jnp.where(place[:, at : at + 1] == column, k, slot)
            found[n, own, :] = slot
        return carry

    def pack(i, carry):
        own = pl.ds(pl.multiple_of(i * 16, 16), 16)
        lane = jnp.where(i * 16 >= half, picks, 0)
        for n, out in enumerate((slot_ref, slot2_ref)):
            slot = found[n, own, :]
            out[own, :] = jnp.where(slot >= 0, slot + lane, slot).astype(F32).astype(BF16)
        return carry

    lax.fori_loop(0, rows // 8, step, 0)
    lax.fori_loop(0, rows // 16, pack, 0)


def pick(low, high, place, chunk, j, y):
    half = place.shape[0]
    here = chunk == j
    low = jnp.where(here, jnp.take_along_axis(y[:half], place, axis=1), low)
    high = jnp.where(here, jnp.take_along_axis(y[half:], place, axis=1), high)
    return low, high


def spread(packed, slot, cols):
    lane = slot[:, cols].astype(F32).astype(jnp.int32)
    half = packed.shape[0]
    value = jnp.concatenate(
        [
            jnp.take_along_axis(packed, jnp.maximum(lane[:half], 0), axis=1),
            jnp.take_along_axis(packed, jnp.maximum(lane[half:], 0), axis=1),
        ],
        axis=0,
    )
    return value, lane >= 0


def sum_of(parts_ref):
    total = parts_ref[0].astype(F32)
    for i in range(1, parts_ref.shape[0]):
        total = total + parts_ref[i].astype(F32)
    return total


def whiten_other_kernel(x_ref, w_ref, out_ref):
    out_ref[...] = jnp.dot(x_ref[...], w_ref[...], preferred_element_type=F32).astype(BF16)


def whiten_own_kernel(x_ref, w_ref, add_ref, out_ref, ready, sems):
    y = jnp.dot(x_ref[...], w_ref[...], preferred_element_type=F32) + add_ref[...].astype(F32)
    ready[...] = y.astype(BF16)
    start(ready, out_ref, sems.at[0]).wait()


def own_bias(at_ref, bias_ref, width):
    return bias_ref[:, pl.ds(pl.multiple_of(at_ref[TOK] * width, width), width)]


def shift_kernel(at_ref, parts_ref, bias_ref, white_ref, out_ref):
    white = sum_of(parts_ref).astype(BF16)
    white_ref[...] = white
    shifted = (white.astype(F32) - own_bias(at_ref, bias_ref, white.shape[1])).astype(BF16)
    for i in range(out_ref.shape[0]):
        out_ref[i] = shifted


def error_kernel(at_ref, parts_ref, bias_ref, white_ref, out_ref):
    rebuilt = sum_of(parts_ref) + own_bias(at_ref, bias_ref, white_ref.shape[1])
    grad = (grad_scale * (rebuilt - white_ref[...].astype(F32))).astype(BF16)
    for i in range(out_ref.shape[0]):
        out_ref[i] = grad


def product_kernel(contract, x_ref, place_ref, w_ref, w2_ref, out_ref, held, sems):
    copy = start(w_ref, held, sems.at[0])
    place = place_ref[...]
    lane, chunk = place & (LANES - 1), place >> 7
    low = high = jnp.zeros(place.shape, F32)
    for n, weight in ((1, w2_ref), (0, held)):
        if n == 0:
            copy.wait()
        y = lax.dot_general(
            x_ref[...], weight[...], (((1,), (contract,)), ((), ())), preferred_element_type=F32
        )
        blocks = y.shape[1] // LANES
        for j in range(blocks):
            part = y[:, j * LANES : (j + 1) * LANES]
            low, high = pick(low, high, lane, chunk, n * blocks + j, part)
    column = lax.broadcasted_iota(jnp.int32, place.shape, 1)
    packed = jnp.where(column < LANES // 2, low, high).astype(BF16)
    for i in range(out_ref.shape[0]):
        out_ref[i] = packed


def spread_codes(packed, slot, bias_ref, codes_ref):
    for j in range(codes_ref.shape[1] // LANES):
        cols = pl.ds(j * LANES, LANES)
        value, there = spread(packed, slot, cols)
        codes_ref[:, cols] = jnp.where(there, value + bias_ref[:, cols], 0.0).astype(BF16)


def decode_kernel(
    parts_ref,
    slot_ref,
    slot2_ref,
    bias_ref,
    bias2_ref,
    w_ref,
    w2_ref,
    packed_ref,
    out_ref,
    codes,
    slots,
    held,
    sems,
):
    found = [start(slot_ref, slots.at[0], sems.at[1]), start(slot2_ref, slots.at[1], sems.at[2])]
    copy = start(w_ref, held, sems.at[0])
    packed = sum_of(parts_ref)
    packed_ref[...] = packed
    for n, bias in enumerate((bias_ref, bias2_ref)):
        found[n].wait()
        spread_codes(packed, slots.at[n], bias, codes.at[n])
    y = jnp.dot(codes[1], w2_ref[...], preferred_element_type=F32)
    copy.wait()
    y = y + jnp.dot(codes[0], held[...], preferred_element_type=F32)
    out_ref[...] = y.astype(BF16)


ROWS_BY_ROWS = (((0,), (0,)), ((), ()))


def codes_kernel(packed_ref, packed2_ref, slot_ref, slot2_ref, bias_ref, out_ref, out2_ref):
    spread_codes(packed_ref[...], slot_ref, bias_ref, out_ref)
    spread_codes(packed2_ref[...], slot2_ref, bias_ref, out2_ref)


def decoder_grad_kernel(codes_ref, codes2_ref, grad_ref, grad2_ref, out_ref):
    y = lax.dot_general(codes_ref[...], grad_ref[...], ROWS_BY_ROWS, preferred_element_type=F32)
    y = y + lax.dot_general(
        codes2_ref[...], grad2_ref[...], ROWS_BY_ROWS, preferred_element_type=F32
    )
    out_ref[...] = y.astype(BF16)


def spread_grad(parts_ref, slot_ref, grad):
    packed = sum_of(parts_ref)
    for j in range(grad.shape[1] // LANES):
        cols = pl.ds(j * LANES, LANES)
        value, there = spread(packed, slot_ref, cols)
        grad[:, cols] = jnp.where(there, value, 0.0).astype(BF16)


def row_sum(at_ref, grad, kept):
    ones = jnp.ones((16, grad.shape[0]), BF16)
    cols = pl.ds(pl.multiple_of(at_ref[TOK] * kept, kept), kept)
    return jnp.dot(ones, grad[:, cols], preferred_element_type=F32)[:1]


def first_grad_kernel(at_ref, parts_ref, slot_ref, x_ref, out_ref, bias_ref, grad):
    spread_grad(parts_ref, slot_ref, grad)
    bias_ref[...] = row_sum(at_ref, grad, bias_ref.shape[1])
    out_ref[...] = lax.dot_general(
        x_ref[...], grad[...], ROWS_BY_ROWS, preferred_element_type=F32
    )


def second_grad_kernel(
    at_ref, parts_ref, slot_ref, x_ref, first_ref, first_bias_ref, out_ref, bias_ref, grad, made, sems
):
    spread_grad(parts_ref, slot_ref, grad)
    bias_ref[...] = first_bias_ref[...] + row_sum(at_ref, grad, bias_ref.shape[1])
    height = made.shape[0] // ROW_BLOCKS
    copies = []
    for b in range(ROW_BLOCKS):
        own = pl.ds(b * height, height)
        y = lax.dot_general(x_ref[:, own], grad[...], ROWS_BY_ROWS, preferred_element_type=F32)
        made[own, :] = (y + first_ref[own, :]).astype(BF16)
        copies.append(start(made.at[own], out_ref.at[own], sems.at[b]))
    for copy in copies:
        copy.wait()


def swap(x):
    return lax.ppermute(x, "core", [(0, 1), (1, 0)])


def exchange(x, axes):
    return lax.all_to_all(x, axes, 0, 0)


def body(
    residual, center, whiten, decoder_bias, encoder_weight, encoder_bias, decoder_weight, chosen
):
    core = lax.axis_index("core")
    width = encoder_weight.shape[0]
    latents = encoder_bias.shape[0]
    rows, picks = chosen.shape[1:]
    inputs = center.shape[0]
    receivers = lax.axis_size(FEATURES)
    column = lax.axis_size(COLUMN)
    chip = (lax.axis_index("yh") * lax.axis_size("z") + lax.axis_index("z")) * 2
    at = jnp.stack(
        [core, lax.axis_index("tok"), (chip + core) * latents, (chip + 1 - core) * latents]
    ).astype(jnp.int32)

    centered = (residual[0].astype(F32) - center).astype(BF16)
    out = jnp.broadcast_to(centered[None], (receivers,) + centered.shape)
    out, listed = lax.optimization_barrier((out, chosen))
    place, wide = call(
        functools.partial(place_kernel, latents),
        (SCALARS, HERE),
        [
            (HERE, spec(rows // 2, LANES, dtype=jnp.int32)),
            (HERE, spec(rows, LANES, dtype=jnp.int32)),
        ],
        (at, listed),
        vmem=SMALL,
    )
    arrived, wide, place = lax.optimization_barrier(
        (exchange(out, ("tok", "section")), wide, place)
    )
    arrived = arrived.reshape(2, rows, inputs)
    own_rows = lax.dynamic_index_in_dim(arrived, core, 0, keepdims=False)
    other_rows = lax.dynamic_index_in_dim(arrived, 1 - core, 0, keepdims=False)
    whiten_cols = lax.dynamic_slice_in_dim(whiten, at[TOK] * width, width, 1)
    flops = 2 * rows * width * inputs
    (part,) = call(
        whiten_other_kernel,
        (HERE, HERE),
        [(HERE, spec(rows, width))],
        (other_rows, whiten_cols),
        (),
        flops,
        vmem=SMALL,
    )
    (part,) = call(
        whiten_own_kernel,
        (HERE, HERE, HERE),
        [(HBM, spec(rows, width))],
        (own_rows, whiten_cols, swap(part)),
        [pltpu.VMEM((rows, width), BF16), COPIES((1,))],
        flops,
        vmem=SMALL,
    )
    shares = (column, rows // column, width)
    share, all_shares = spec(*shares[1:]), spec(*shares)
    bias_row, decoder_bias = encoder_bias[None], decoder_bias[None]

    part, wide, encoder_weight, decoder_weight, bias_row = lax.optimization_barrier(
        (part, wide, encoder_weight, decoder_weight, bias_row)
    )
    encoder_weight2, decoder_weight2 = swap(encoder_weight), swap(decoder_weight)
    bias_row2 = swap(bias_row)
    slot, slot2 = call(
        find_kernel,
        (HERE,),
        [(HERE, spec(rows, latents)), (HERE, spec(rows, latents))],
        (wide,),
        [pltpu.VMEM((2, rows, latents), jnp.int32)],
        4 * picks * rows * latents,
    )
    parts, slot, slot2, bias_row2 = lax.optimization_barrier(
        (exchange(part.reshape(shares), COLUMN), slot, slot2, bias_row2)
    )
    whitened, out = call(
        shift_kernel,
        (SCALARS, HERE, HERE),
        [(HERE, share), (HERE, all_shares)],
        (at, parts, decoder_bias),
        vmem=SMALL,
    )
    out, weight, weight2 = lax.optimization_barrier((out, encoder_weight, encoder_weight2))
    weight, weight2 = swap(weight2), swap(weight)
    shifted = exchange(out, COLUMN).reshape(rows, width)

    flops = 4 * rows * width * latents
    moved = 4 * width * latents
    weight_held = [pltpu.VMEM((width, latents), BF16), COPIES((1,))]

    def chosen_product(contract, x, weight, weight2):
        (packed,) = call(
            functools.partial(product_kernel, contract),
            (HERE, HERE, ANY, HERE),
            [(HERE, spec(receivers, rows // 2, LANES))],
            (x, place, weight, weight2),
            weight_held,
            flops,
            moved,
            MOST,
        )
        return packed

    encoded = chosen_product(0, shifted, weight, weight2)
    encoded, shifted, weight, weight2 = lax.optimization_barrier(
        (encoded, shifted, decoder_weight, decoder_weight2)
    )
    weight, weight2 = swap(weight2), swap(weight)
    shifted2, other_slot = swap(shifted), swap(slot2)
    encoded = exchange(encoded, FEATURES)
    packed, part = call(
        decode_kernel,
        (HERE, ANY, ANY, HERE, HERE, ANY, HERE),
        [(HERE, spec(rows // 2, LANES, dtype=F32)), (HERE, spec(rows, width))],
        (encoded, slot, slot2, bias_row, bias_row2, weight, weight2),
        [
            pltpu.VMEM((2, rows, latents), BF16),
            pltpu.VMEM((2, rows, latents), BF16),
            pltpu.VMEM((latents, width), BF16),
            COPIES((3,)),
        ],
        flops,
        moved,
        MOST,
    )
    part, packed = lax.optimization_barrier((part, packed))
    codes, codes2 = call(
        codes_kernel,
        (HERE,) * 5,
        [(HERE, spec(rows, latents)), (HERE, spec(rows, latents))],
        (packed, swap(packed), slot, other_slot, bias_row),
    )
    parts, codes, codes2, shifted2, other_slot = lax.optimization_barrier(
        (exchange(part.reshape(shares), COLUMN), codes, codes2, shifted2, other_slot)
    )
    (out,) = call(
        error_kernel,
        (SCALARS, HERE, HERE, HERE),
        [(HERE, all_shares)],
        (at, parts, decoder_bias, whitened),
        vmem=SMALL,
    )
    out, weight, weight2 = lax.optimization_barrier((out, decoder_weight, decoder_weight2))
    weight, weight2 = swap(weight2), swap(weight)
    grad = exchange(out, COLUMN).reshape(rows, width)

    packed = chosen_product(1, grad, weight, weight2)
    packed, grad = lax.optimization_barrier((packed, grad))
    (decoder_grad,) = call(
        decoder_grad_kernel,
        (HERE,) * 4,
        [(HERE, spec(latents, width))],
        (codes, codes2, grad, swap(grad)),
        (),
        flops,
        moved,
    )
    code_grad, decoder_grad = lax.optimization_barrier(
        (exchange(packed, FEATURES), decoder_grad)
    )
    code_grad2 = swap(code_grad)
    bias_half = spec(1, latents // 2, dtype=F32)
    first_grad, first_bias = call(
        first_grad_kernel,
        (SCALARS, HERE, HERE, HERE),
        [(HERE, spec(width, latents, dtype=F32)), (HERE, bias_half)],
        (at, code_grad, slot, shifted),
        [pltpu.VMEM((rows, latents), BF16)],
        flops,
        moved,
        MIDDLE,
    )
    encoder_grad, bias_grad = call(
        second_grad_kernel,
        (SCALARS, HERE, HERE, HERE, HERE, HERE),
        [(ANY, spec(width, latents)), (HERE, bias_half)],
        (at, code_grad2, other_slot, shifted2, first_grad, first_bias),
        [
            pltpu.VMEM((rows, latents), BF16),
            pltpu.VMEM((width, latents), BF16),
            COPIES((ROW_BLOCKS,)),
        ],
        flops,
        moved,
        MIDDLE,
    )
    return encoder_grad, decoder_grad, bias_grad[0]


def solution(mesh):
    fine = Mesh(mesh.devices.reshape(4, 2, 8, 2, 2), ("section", "yh", "z", "core", "tok"))
    lat = ("yh", "z", "core")
    return jax.shard_map(
        body,
        mesh=fine,
        in_specs=(
            P("tok", "section", lat),
            P(lat),
            P(lat, "section"),
            P("section"),
            P(("section", "tok"), lat),
            P(lat),
            P(lat, ("section", "tok")),
            P(),
        ),
        out_specs=(P(("section", "tok"), lat), P(lat, ("section", "tok")), P(lat + ("tok",))),
        check_vma=False,
    )
```

```python
import functools

import jax
import jax.numpy as jnp
from jax import lax
from jax.experimental import pallas as pl
from jax.experimental.pallas import tpu as pltpu
from jax.sharding import Mesh
from jax.sharding import PartitionSpec as P

grad_scale = 0.125
LANES = 128
F32 = jnp.float32
BF16 = jnp.bfloat16
HERE = pl.BlockSpec(memory_space=pltpu.VMEM)
SCALARS = pl.BlockSpec(memory_space=pltpu.SMEM)
ANY = pl.BlockSpec(memory_space=pl.ANY)
HBM = pl.BlockSpec(memory_space=pltpu.HBM)
MIB = 1024 * 1024
SMALL, MIDDLE, MOST = 12, 24, 24
COPIES = pltpu.SemaphoreType.DMA
ROW_BLOCKS = 8
FEATURES = ("section", "tok")
COLUMN = ("yh", "z")
CORE, TOK, FIRST, FIRST2 = range(4)


def spec(*shape, dtype=BF16):
    return jax.ShapeDtypeStruct(shape, dtype)


def call(kernel, ins, outs, operands, scratch=(), flops=0, moved=2**20, vmem=60):
    return pl.pallas_call(
        kernel,
        in_specs=list(ins),
        out_specs=tuple(place for place, _ in outs),
        out_shape=tuple(shape for _, shape in outs),
        scratch_shapes=list(scratch),
        compiler_params=pltpu.CompilerParams(vmem_limit_bytes=vmem * MIB),
        cost_estimate=pl.CostEstimate(flops=flops, bytes_accessed=moved, transcendentals=0),
    )(*operands)


def start(source, target, sem):
    copy = pltpu.make_async_copy(source, target, sem)
    copy.start()
    return copy


def place_kernel(latents, at_ref, chosen_ref, packed_ref, wide_ref):
    picked = chosen_ref[at_ref[CORE]]
    own, other = picked - at_ref[FIRST], picked - at_ref[FIRST2]
    wide_ref[...] = jnp.concatenate([own, other], axis=1)
    place = jnp.where((other >= 0) & (other < latents), other + latents, -1)
    place = jnp.where((own >= 0) & (own < latents), own, place)
    half = place.shape[0] // 2
    packed_ref[...] = jnp.concatenate([place[:half], place[half:]], axis=1)


def find_kernel(wide_ref, slot_ref, slot2_ref, found):
    rows, width = slot_ref.shape
    half, picks = rows // 2, LANES // 2
    column = lax.broadcasted_iota(jnp.int32, (8, width), 1)

    def step(base, i, carry):
        own = pl.ds(pl.multiple_of(i * 8, 8), 8)
        place = wide_ref[own, :]
        for n in range(2):
            slot = jnp.full((8, width), -1, jnp.int32)
            for k in range(picks):
                at = n * picks + k
                slot = jnp.where(place[:, at : at + 1] == column, base + k, slot)
            found[n, own, :] = slot
        return carry

    def pack(i, carry):
        own = pl.ds(pl.multiple_of(i * 16, 16), 16)
        for n, out in enumerate((slot_ref, slot2_ref)):
            out[own, :] = found[n, own, :].astype(F32).astype(BF16)
        return carry

    lax.fori_loop(0, half // 8, functools.partial(step, 0), 0)
    lax.fori_loop(half // 8, rows // 8, functools.partial(step, picks), 0)
    lax.fori_loop(0, rows // 16, pack, 0)


def pick(low, high, place, chunk, j, y):
    half = place.shape[0]
    here = chunk == j
    low = jnp.where(here, jnp.take_along_axis(y[:half], place, axis=1), low)
    high = jnp.where(here, jnp.take_along_axis(y[half:], place, axis=1), high)
    return low, high


def spread(packed, slot, cols):
    lane = slot[:, cols].astype(F32).astype(jnp.int32)
    half = packed.shape[0]
    value = jnp.concatenate(
        [
            jnp.take_along_axis(packed, jnp.maximum(lane[:half], 0), axis=1),
            jnp.take_along_axis(packed, jnp.maximum(lane[half:], 0), axis=1),
        ],
        axis=0,
    )
    return value, lane >= 0


def sum_of(parts_ref):
    total = parts_ref[0].astype(F32)
    for i in range(1, parts_ref.shape[0]):
        total = total + parts_ref[i].astype(F32)
    return total


def whiten_other_kernel(x_ref, w_ref, out_ref):
    out_ref[...] = jnp.dot(x_ref[...], w_ref[...], preferred_element_type=F32).astype(BF16)


def whiten_own_kernel(x_ref, w_ref, add_ref, out_ref, ready, sems):
    y = jnp.dot(x_ref[...], w_ref[...], preferred_element_type=F32) + add_ref[...].astype(F32)
    ready[...] = y.astype(BF16)
    start(ready, out_ref, sems.at[0]).wait()


def own_bias(at_ref, bias_ref, width):
    return bias_ref[:, pl.ds(pl.multiple_of(at_ref[TOK] * width, width), width)]


def shift_kernel(at_ref, parts_ref, bias_ref, white_ref, out_ref):
    white = sum_of(parts_ref).astype(BF16)
    white_ref[...] = white
    shifted = (white.astype(F32) - own_bias(at_ref, bias_ref, white.shape[1])).astype(BF16)
    for i in range(out_ref.shape[0]):
        out_ref[i] = shifted


def error_kernel(at_ref, parts_ref, bias_ref, white_ref, out_ref):
    rebuilt = sum_of(parts_ref) + own_bias(at_ref, bias_ref, white_ref.shape[1])
    grad = (grad_scale * (rebuilt - white_ref[...].astype(F32))).astype(BF16)
    for i in range(out_ref.shape[0]):
        out_ref[i] = grad


def product_kernel(contract, x_ref, place_ref, w_ref, w2_ref, out_ref):
    place = place_ref[...]
    lane, chunk = place & (LANES - 1), place >> 7
    low = high = jnp.zeros(place.shape, F32)
    for n, weight in enumerate((w_ref, w2_ref)):
        y = lax.dot_general(
            x_ref[...], weight[...], (((1,), (contract,)), ((), ())), preferred_element_type=F32
        )
        blocks = y.shape[1] // LANES
        for j in range(blocks):
            part = y[:, j * LANES : (j + 1) * LANES]
            low, high = pick(low, high, lane, chunk, n * blocks + j, part)
    column = lax.broadcasted_iota(jnp.int32, place.shape, 1)
    packed = jnp.where(column < LANES // 2, low, high).astype(BF16)
    for i in range(out_ref.shape[0]):
        out_ref[i] = packed


def spread_codes(packed, slot, bias_ref, codes_ref):
    for j in range(codes_ref.shape[1] // LANES):
        cols = pl.ds(j * LANES, LANES)
        value, there = spread(packed, slot, cols)
        codes_ref[:, cols] = jnp.where(there, value + bias_ref[:, cols], 0.0).astype(BF16)


def decode_kernel(
    parts_ref, slot_ref, slot2_ref, bias_ref, bias2_ref, w_ref, w2_ref, packed_ref, out_ref, codes
):
    packed = sum_of(parts_ref)
    packed_ref[...] = packed
    spread_codes(packed, slot_ref, bias_ref, codes.at[0])
    spread_codes(packed, slot2_ref, bias2_ref, codes.at[1])
    y = jnp.dot(codes[0], w_ref[...], preferred_element_type=F32)
    y = y + jnp.dot(codes[1], w2_ref[...], preferred_element_type=F32)
    out_ref[...] = y.astype(BF16)


ROWS_BY_ROWS = (((0,), (0,)), ((), ()))


def codes_kernel(packed_ref, packed2_ref, slot_ref, slot2_ref, bias_ref, out_ref, out2_ref):
    spread_codes(packed_ref[...], slot_ref, bias_ref, out_ref)
    spread_codes(packed2_ref[...], slot2_ref, bias_ref, out2_ref)


def decoder_grad_kernel(codes_ref, codes2_ref, grad_ref, grad2_ref, out_ref):
    y = lax.dot_general(codes_ref[...], grad_ref[...], ROWS_BY_ROWS, preferred_element_type=F32)
    y = y + lax.dot_general(
        codes2_ref[...], grad2_ref[...], ROWS_BY_ROWS, preferred_element_type=F32
    )
    out_ref[...] = y.astype(BF16)


def spread_grad(parts_ref, slot_ref, grad):
    packed = sum_of(parts_ref)
    for j in range(grad.shape[1] // LANES):
        cols = pl.ds(j * LANES, LANES)
        value, there = spread(packed, slot_ref, cols)
        grad[:, cols] = jnp.where(there, value, 0.0).astype(BF16)


def row_sum(at_ref, grad, kept):
    ones = jnp.ones((16, grad.shape[0]), BF16)
    cols = pl.ds(pl.multiple_of(at_ref[TOK] * kept, kept), kept)
    return jnp.dot(ones, grad[:, cols], preferred_element_type=F32)[:1]


def first_grad_kernel(at_ref, parts_ref, slot_ref, x_ref, out_ref, bias_ref, grad):
    spread_grad(parts_ref, slot_ref, grad)
    bias_ref[...] = row_sum(at_ref, grad, bias_ref.shape[1])
    out_ref[...] = lax.dot_general(
        x_ref[...], grad[...], ROWS_BY_ROWS, preferred_element_type=F32
    )


def second_grad_kernel(
    at_ref, parts_ref, slot_ref, x_ref, first_ref, first_bias_ref, out_ref, bias_ref, grad, made, sems
):
    spread_grad(parts_ref, slot_ref, grad)
    bias_ref[...] = first_bias_ref[...] + row_sum(at_ref, grad, bias_ref.shape[1])
    height = made.shape[0] // ROW_BLOCKS
    copies = []
    for b in range(ROW_BLOCKS):
        own = pl.ds(b * height, height)
        y = lax.dot_general(x_ref[:, own], grad[...], ROWS_BY_ROWS, preferred_element_type=F32)
        made[own, :] = (y + first_ref[own, :]).astype(BF16)
        copies.append(start(made.at[own], out_ref.at[own], sems.at[b]))
    for copy in copies:
        copy.wait()


def swap(x):
    return lax.ppermute(x, "core", [(0, 1), (1, 0)])


def exchange(x, axes):
    return lax.all_to_all(x, axes, 0, 0)


def body(
    residual, center, whiten, decoder_bias, encoder_weight, encoder_bias, decoder_weight, chosen
):
    core = lax.axis_index("core")
    width = encoder_weight.shape[0]
    latents = encoder_bias.shape[0]
    rows, picks = chosen.shape[1:]
    inputs = center.shape[0]
    receivers = lax.axis_size(FEATURES)
    column = lax.axis_size(COLUMN)
    chip = (lax.axis_index("yh") * lax.axis_size("z") + lax.axis_index("z")) * 2
    at = jnp.stack(
        [core, lax.axis_index("tok"), (chip + core) * latents, (chip + 1 - core) * latents]
    ).astype(jnp.int32)

    centered = (residual[0].astype(F32) - center).astype(BF16)
    out = jnp.broadcast_to(centered[None], (receivers,) + centered.shape)
    out, listed = lax.optimization_barrier((out, chosen))
    place, wide = call(
        functools.partial(place_kernel, latents),
        (SCALARS, HERE),
        [
            (HERE, spec(rows // 2, LANES, dtype=jnp.int32)),
            (HERE, spec(rows, LANES, dtype=jnp.int32)),
        ],
        (at, listed),
        vmem=SMALL,
    )
    arrived, wide, place = lax.optimization_barrier(
        (exchange(out, ("tok", "section")), wide, place)
    )
    arrived = arrived.reshape(2, rows, inputs)
    own_rows = lax.dynamic_index_in_dim(arrived, core, 0, keepdims=False)
    other_rows = lax.dynamic_index_in_dim(arrived, 1 - core, 0, keepdims=False)
    whiten_cols = lax.dynamic_slice_in_dim(whiten, at[TOK] * width, width, 1)
    flops = 2 * rows * width * inputs
    (part,) = call(
        whiten_other_kernel,
        (HERE, HERE),
        [(HERE, spec(rows, width))],
        (other_rows, whiten_cols),
        (),
        flops,
        vmem=SMALL,
    )
    (part,) = call(
        whiten_own_kernel,
        (HERE, HERE, HERE),
        [(HBM, spec(rows, width))],
        (own_rows, whiten_cols, swap(part)),
        [pltpu.VMEM((rows, width), BF16), COPIES((1,))],
        flops,
        vmem=SMALL,
    )
    shares = (column, rows // column, width)
    share, all_shares = spec(*shares[1:]), spec(*shares)
    bias_row, decoder_bias = encoder_bias[None], decoder_bias[None]

    part, wide, encoder_weight, decoder_weight, bias_row = lax.optimization_barrier(
        (part, wide, encoder_weight, decoder_weight, bias_row)
    )
    encoder_weight2, decoder_weight2 = swap(encoder_weight), swap(decoder_weight)
    bias_row2 = swap(bias_row)
    slot, slot2 = call(
        find_kernel,
        (HERE,),
        [(HERE, spec(rows, latents)), (HERE, spec(rows, latents))],
        (wide,),
        [pltpu.VMEM((2, rows, latents), jnp.int32)],
        4 * picks * rows * latents,
    )
    parts, slot, slot2, bias_row2 = lax.optimization_barrier(
        (exchange(part.reshape(shares), COLUMN), slot, slot2, bias_row2)
    )
    whitened, out = call(
        shift_kernel,
        (SCALARS, HERE, HERE),
        [(HERE, share), (HERE, all_shares)],
        (at, parts, decoder_bias),
        vmem=SMALL,
    )
    out, weight, weight2 = lax.optimization_barrier((out, encoder_weight, encoder_weight2))
    weight, weight2 = swap(weight2), swap(weight)
    shifted = exchange(out, COLUMN).reshape(rows, width)

    flops = 4 * rows * width * latents
    moved = 4 * width * latents

    def chosen_product(contract, x, weight, weight2):
        (packed,) = call(
            functools.partial(product_kernel, contract),
            (HERE, HERE, HERE, HERE),
            [(HERE, spec(receivers, rows // 2, LANES))],
            (x, place, weight, weight2),
            (),
            flops,
            moved,
            MOST,
        )
        return packed

    encoded = chosen_product(0, shifted, weight, weight2)
    encoded, shifted, weight, weight2 = lax.optimization_barrier(
        (encoded, shifted, decoder_weight, decoder_weight2)
    )
    weight, weight2 = swap(weight2), swap(weight)
    shifted2, other_slot = swap(shifted), swap(slot2)
    encoded = exchange(encoded, FEATURES)
    packed, part = call(
        decode_kernel,
        (HERE,) * 7,
        [(HERE, spec(rows // 2, LANES, dtype=F32)), (HERE, spec(rows, width))],
        (encoded, slot, slot2, bias_row, bias_row2, weight, weight2),
        [pltpu.VMEM((2, rows, latents), BF16)],
        flops,
        moved,
        MOST,
    )
    part, packed = lax.optimization_barrier((part, packed))
    codes, codes2 = call(
        codes_kernel,
        (HERE,) * 5,
        [(HERE, spec(rows, latents)), (HERE, spec(rows, latents))],
        (packed, swap(packed), slot, other_slot, bias_row),
    )
    parts, codes, codes2, shifted2, other_slot = lax.optimization_barrier(
        (exchange(part.reshape(shares), COLUMN), codes, codes2, shifted2, other_slot)
    )
    (out,) = call(
        error_kernel,
        (SCALARS, HERE, HERE, HERE),
        [(HERE, all_shares)],
        (at, parts, decoder_bias, whitened),
        vmem=SMALL,
    )
    out, weight, weight2 = lax.optimization_barrier((out, decoder_weight, decoder_weight2))
    weight, weight2 = swap(weight2), swap(weight)
    grad = exchange(out, COLUMN).reshape(rows, width)

    packed = chosen_product(1, grad, weight, weight2)
    packed, grad = lax.optimization_barrier((packed, grad))
    (decoder_grad,) = call(
        decoder_grad_kernel,
        (HERE,) * 4,
        [(HERE, spec(latents, width))],
        (codes, codes2, grad, swap(grad)),
        (),
        flops,
        moved,
    )
    code_grad, decoder_grad = lax.optimization_barrier(
        (exchange(packed, FEATURES), decoder_grad)
    )
    code_grad2 = swap(code_grad)
    bias_half = spec(1, latents // 2, dtype=F32)
    first_grad, first_bias = call(
        first_grad_kernel,
        (SCALARS, HERE, HERE, HERE),
        [(HERE, spec(width, latents, dtype=F32)), (HERE, bias_half)],
        (at, code_grad, slot, shifted),
        [pltpu.VMEM((rows, latents), BF16)],
        flops,
        moved,
        MIDDLE,
    )
    encoder_grad, bias_grad = call(
        second_grad_kernel,
        (SCALARS, HERE, HERE, HERE, HERE, HERE),
        [(ANY, spec(width, latents)), (HERE, bias_half)],
        (at, code_grad2, other_slot, shifted2, first_grad, first_bias),
        [
            pltpu.VMEM((rows, latents), BF16),
            pltpu.VMEM((width, latents), BF16),
            COPIES((ROW_BLOCKS,)),
        ],
        flops,
        moved,
        MIDDLE,
    )
    return encoder_grad, decoder_grad, bias_grad[0]


def solution(mesh):
    fine = Mesh(mesh.devices.reshape(4, 2, 8, 2, 2), ("section", "yh", "z", "core", "tok"))
    lat = ("yh", "z", "core")
    return jax.shard_map(
        body,
        mesh=fine,
        in_specs=(
            P("tok", "section", lat),
            P(lat),
            P(lat, "section"),
            P("section"),
            P(("section", "tok"), lat),
            P(lat),
            P(lat, ("section", "tok")),
            P(),
        ),
        out_specs=(P(("section", "tok"), lat), P(lat, ("section", "tok")), P(lat + ("tok",))),
        check_vma=False,
    )
```

```python
import functools

import jax
import jax.numpy as jnp
from jax import lax
from jax.experimental import pallas as pl
from jax.experimental.pallas import tpu as pltpu
from jax.sharding import Mesh
from jax.sharding import PartitionSpec as P

grad_scale = 0.125
LANES = 128
F32 = jnp.float32
BF16 = jnp.bfloat16
HERE = pl.BlockSpec(memory_space=pltpu.VMEM)
SCALARS = pl.BlockSpec(memory_space=pltpu.SMEM)
ANY = pl.BlockSpec(memory_space=pl.ANY)
HBM = pl.BlockSpec(memory_space=pltpu.HBM)
MIB = 1024 * 1024
SMALL, MIDDLE, MOST = 12, 24, 24
COPIES = pltpu.SemaphoreType.DMA
ROW_BLOCKS = 8
EARLY_ROWS = 32
FEATURES = ("section", "tok")
COLUMN = ("yh", "z")
CORE, TOK, FIRST, FIRST2 = range(4)


def spec(*shape, dtype=BF16):
    return jax.ShapeDtypeStruct(shape, dtype)


def call(kernel, ins, outs, operands, scratch=(), flops=0, moved=2**20, vmem=60):
    return pl.pallas_call(
        kernel,
        in_specs=list(ins),
        out_specs=tuple(place for place, _ in outs),
        out_shape=tuple(shape for _, shape in outs),
        scratch_shapes=list(scratch),
        compiler_params=pltpu.CompilerParams(vmem_limit_bytes=vmem * MIB),
        cost_estimate=pl.CostEstimate(flops=flops, bytes_accessed=moved, transcendentals=0),
    )(*operands)


def start(source, target, sem):
    copy = pltpu.make_async_copy(source, target, sem)
    copy.start()
    return copy


def place_kernel(latents, at_ref, chosen_ref, packed_ref, wide_ref):
    picked = chosen_ref[at_ref[CORE]]
    own, other = picked - at_ref[FIRST], picked - at_ref[FIRST2]
    wide_ref[...] = jnp.concatenate([own, other], axis=1)
    place = jnp.where((other >= 0) & (other < latents), other + latents, -1)
    place = jnp.where((own >= 0) & (own < latents), own, place)
    half = place.shape[0] // 2
    packed_ref[...] = jnp.concatenate([place[:half], place[half:]], axis=1)


def find_kernel(done, wide_ref, *refs):
    given, (slot_ref, slot2_ref, found) = refs[:-3], refs[-3:]
    rows, width = slot_ref.shape
    half, picks = wide_ref.shape[0] // 2, LANES // 2
    column = lax.broadcasted_iota(jnp.int32, (8, width), 1)

    def step(base, i, carry):
        own = pl.ds(pl.multiple_of(i * 8, 8), 8)
        place = wide_ref[own, :]
        for n in range(2):
            slot = jnp.full((8, width), -1, jnp.int32)
            for k in range(picks):
                at = n * picks + k
                slot = jnp.where(place[:, at : at + 1] == column, base + k, slot)
            found[n, own, :] = slot
        return carry

    def pack(i, carry):
        own = pl.ds(pl.multiple_of(i * 16, 16), 16)
        for n, out in enumerate((slot_ref, slot2_ref)):
            out[own, :] = found[n, own, :].astype(F32).astype(BF16)
        return carry

    for before, out in zip(given, (slot_ref, slot2_ref)):
        out[:done, :] = before[...]
    lax.fori_loop(done // 8, min(rows, half) // 8, functools.partial(step, 0), 0)
    if rows > half:
        lax.fori_loop(half // 8, rows // 8, functools.partial(step, picks), 0)
    lax.fori_loop(done // 16, rows // 16, pack, 0)


def pick(low, high, place, chunk, j, y):
    half = place.shape[0]
    here = chunk == j
    low = jnp.where(here, jnp.take_along_axis(y[:half], place, axis=1), low)
    high = jnp.where(here, jnp.take_along_axis(y[half:], place, axis=1), high)
    return low, high


def spread(packed, slot, cols):
    lane = slot[:, cols].astype(F32).astype(jnp.int32)
    half = packed.shape[0]
    value = jnp.concatenate(
        [
            jnp.take_along_axis(packed, jnp.maximum(lane[:half], 0), axis=1),
            jnp.take_along_axis(packed, jnp.maximum(lane[half:], 0), axis=1),
        ],
        axis=0,
    )
    return value, lane >= 0


def sum_of(parts_ref):
    total = parts_ref[0].astype(F32)
    for i in range(1, parts_ref.shape[0]):
        total = total + parts_ref[i].astype(F32)
    return total


def whiten_kernel(x_ref, w_ref, x2_ref, w2_ref, out_ref, ready, sems):
    y = jnp.dot(x_ref[...], w_ref[...], preferred_element_type=F32)
    y = y + jnp.dot(x2_ref[...], w2_ref[...], preferred_element_type=F32)
    ready[...] = y.astype(BF16)
    start(ready, out_ref, sems.at[0]).wait()


def own_bias(at_ref, bias_ref, width):
    return bias_ref[:, pl.ds(pl.multiple_of(at_ref[TOK] * width, width), width)]


def shift_kernel(at_ref, parts_ref, bias_ref, white_ref, out_ref):
    white = sum_of(parts_ref).astype(BF16)
    white_ref[...] = white
    shifted = (white.astype(F32) - own_bias(at_ref, bias_ref, white.shape[1])).astype(BF16)
    for i in range(out_ref.shape[0]):
        out_ref[i] = shifted


def error_kernel(at_ref, parts_ref, bias_ref, white_ref, out_ref):
    rebuilt = sum_of(parts_ref) + own_bias(at_ref, bias_ref, white_ref.shape[1])
    grad = (grad_scale * (rebuilt - white_ref[...].astype(F32))).astype(BF16)
    for i in range(out_ref.shape[0]):
        out_ref[i] = grad


def product_kernel(contract, x_ref, place_ref, w_ref, w2_ref, out_ref):
    place = place_ref[...]
    lane, chunk = place & (LANES - 1), place >> 7
    low = high = jnp.zeros(place.shape, F32)
    for n, weight in enumerate((w_ref, w2_ref)):
        y = lax.dot_general(
            x_ref[...], weight[...], (((1,), (contract,)), ((), ())), preferred_element_type=F32
        )
        blocks = y.shape[1] // LANES
        for j in range(blocks):
            part = y[:, j * LANES : (j + 1) * LANES]
            low, high = pick(low, high, lane, chunk, n * blocks + j, part)
    column = lax.broadcasted_iota(jnp.int32, place.shape, 1)
    packed = jnp.where(column < LANES // 2, low, high).astype(BF16)
    for i in range(out_ref.shape[0]):
        out_ref[i] = packed


def spread_codes(packed, slot, bias_ref, codes_ref):
    for j in range(codes_ref.shape[1] // LANES):
        cols = pl.ds(j * LANES, LANES)
        value, there = spread(packed, slot, cols)
        codes_ref[:, cols] = jnp.where(there, value + bias_ref[:, cols], 0.0).astype(BF16)


def decode_kernel(
    parts_ref, slot_ref, slot2_ref, bias_ref, bias2_ref, w_ref, w2_ref, packed_ref, out_ref, codes
):
    packed = sum_of(parts_ref)
    packed_ref[...] = packed
    spread_codes(packed, slot_ref, bias_ref, codes.at[0])
    spread_codes(packed, slot2_ref, bias2_ref, codes.at[1])
    y = jnp.dot(codes[0], w_ref[...], preferred_element_type=F32)
    y = y + jnp.dot(codes[1], w2_ref[...], preferred_element_type=F32)
    out_ref[...] = y.astype(BF16)


ROWS_BY_ROWS = (((0,), (0,)), ((), ()))


def codes_kernel(packed_ref, packed2_ref, slot_ref, slot2_ref, bias_ref, out_ref, out2_ref):
    spread_codes(packed_ref[...], slot_ref, bias_ref, out_ref)
    spread_codes(packed2_ref[...], slot2_ref, bias_ref, out2_ref)


def decoder_grad_kernel(codes_ref, codes2_ref, grad_ref, grad2_ref, out_ref):
    y = lax.dot_general(codes_ref[...], grad_ref[...], ROWS_BY_ROWS, preferred_element_type=F32)
    y = y + lax.dot_general(
        codes2_ref[...], grad2_ref[...], ROWS_BY_ROWS, preferred_element_type=F32
    )
    out_ref[...] = y.astype(BF16)


def spread_grad(parts_ref, slot_ref, grad):
    packed = sum_of(parts_ref)
    for j in range(grad.shape[1] // LANES):
        cols = pl.ds(j * LANES, LANES)
        value, there = spread(packed, slot_ref, cols)
        grad[:, cols] = jnp.where(there, value, 0.0).astype(BF16)


def row_sum(at_ref, grad, kept):
    ones = jnp.ones((16, grad.shape[0]), BF16)
    cols = pl.ds(pl.multiple_of(at_ref[TOK] * kept, kept), kept)
    return jnp.dot(ones, grad[:, cols], preferred_element_type=F32)[:1]


def first_grad_kernel(at_ref, parts_ref, slot_ref, x_ref, out_ref, bias_ref, grad):
    spread_grad(parts_ref, slot_ref, grad)
    bias_ref[...] = row_sum(at_ref, grad, bias_ref.shape[1])
    out_ref[...] = lax.dot_general(
        x_ref[...], grad[...], ROWS_BY_ROWS, preferred_element_type=F32
    )


def second_grad_kernel(
    at_ref, parts_ref, slot_ref, x_ref, first_ref, first_bias_ref, out_ref, bias_ref, grad, made, sems
):
    spread_grad(parts_ref, slot_ref, grad)
    bias_ref[...] = first_bias_ref[...] + row_sum(at_ref, grad, bias_ref.shape[1])
    height = made.shape[0] // ROW_BLOCKS
    copies = []
    for b in range(ROW_BLOCKS):
        own = pl.ds(b * height, height)
        y = lax.dot_general(x_ref[:, own], grad[...], ROWS_BY_ROWS, preferred_element_type=F32)
        made[own, :] = (y + first_ref[own, :]).astype(BF16)
        copies.append(start(made.at[own], out_ref.at[own], sems.at[b]))
    for copy in copies:
        copy.wait()


def swap(x):
    return lax.ppermute(x, "core", [(0, 1), (1, 0)])


def exchange(x, axes):
    return lax.all_to_all(x, axes, 0, 0)


def body(
    residual, center, whiten, decoder_bias, encoder_weight, encoder_bias, decoder_weight, chosen
):
    core = lax.axis_index("core")
    width = encoder_weight.shape[0]
    latents = encoder_bias.shape[0]
    rows, picks = chosen.shape[1:]
    inputs = center.shape[0]
    receivers = lax.axis_size(FEATURES)
    column = lax.axis_size(COLUMN)
    chip = (lax.axis_index("yh") * lax.axis_size("z") + lax.axis_index("z")) * 2
    at = jnp.stack(
        [core, lax.axis_index("tok"), (chip + core) * latents, (chip + 1 - core) * latents]
    ).astype(jnp.int32)

    centered = (residual[0].astype(F32) - center).astype(BF16)
    out = jnp.broadcast_to(centered[None], (receivers,) + centered.shape)
    whiten_cols = lax.dynamic_slice_in_dim(whiten, at[TOK] * width, width, 1)
    out, listed, whiten_cols = lax.optimization_barrier((out, chosen, whiten_cols))
    place, wide = call(
        functools.partial(place_kernel, latents),
        (SCALARS, HERE),
        [
            (HERE, spec(rows // 2, LANES, dtype=jnp.int32)),
            (HERE, spec(rows, LANES, dtype=jnp.int32)),
        ],
        (at, listed),
        vmem=SMALL,
    )

    def find(done, count, operands):
        return call(
            functools.partial(find_kernel, done),
            (HERE,) * len(operands),
            [(HERE, spec(count, latents))] * 2,
            operands,
            [pltpu.VMEM((2, count, latents), jnp.int32)],
            4 * picks * (count - done) * latents,
        )

    early = find(0, EARLY_ROWS, (wide,))
    whiten_cols2 = swap(whiten_cols)
    arrived, wide, place, early = lax.optimization_barrier(
        (exchange(out, ("tok", "section")), wide, place, early)
    )
    arrived = arrived.reshape(2, rows, inputs)
    own_rows = lax.dynamic_index_in_dim(arrived, core, 0, keepdims=False)
    other_rows = lax.dynamic_index_in_dim(arrived, 1 - core, 0, keepdims=False)
    (part,) = call(
        whiten_kernel,
        (HERE,) * 4,
        [(HBM, spec(rows, width))],
        (own_rows, whiten_cols, swap(other_rows), whiten_cols2),
        [pltpu.VMEM((rows, width), BF16), COPIES((1,))],
        4 * rows * width * inputs,
        vmem=SMALL,
    )
    shares = (column, rows // column, width)
    share, all_shares = spec(*shares[1:]), spec(*shares)
    bias_row, decoder_bias = encoder_bias[None], decoder_bias[None]

    part, wide, encoder_weight, decoder_weight, bias_row = lax.optimization_barrier(
        (part, wide, encoder_weight, decoder_weight, bias_row)
    )
    encoder_weight2, decoder_weight2 = swap(encoder_weight), swap(decoder_weight)
    bias_row2 = swap(bias_row)
    slot, slot2 = find(EARLY_ROWS, rows, (wide, *early))
    parts, slot, slot2, bias_row2 = lax.optimization_barrier(
        (exchange(part.reshape(shares), COLUMN), slot, slot2, bias_row2)
    )
    whitened, out = call(
        shift_kernel,
        (SCALARS, HERE, HERE),
        [(HERE, share), (HERE, all_shares)],
        (at, parts, decoder_bias),
        vmem=SMALL,
    )
    out, weight, weight2 = lax.optimization_barrier((out, encoder_weight, encoder_weight2))
    weight, weight2 = swap(weight2), swap(weight)
    shifted = exchange(out, COLUMN).reshape(rows, width)

    flops = 4 * rows * width * latents
    moved = 4 * width * latents

    def chosen_product(contract, x, weight, weight2):
        (packed,) = call(
            functools.partial(product_kernel, contract),
            (HERE, HERE, HERE, HERE),
            [(HERE, spec(receivers, rows // 2, LANES))],
            (x, place, weight, weight2),
            (),
            flops,
            moved,
            MOST,
        )
        return packed

    encoded = chosen_product(0, shifted, weight, weight2)
    encoded, shifted, weight, weight2 = lax.optimization_barrier(
        (encoded, shifted, decoder_weight, decoder_weight2)
    )
    weight, weight2 = swap(weight2), swap(weight)
    shifted2, other_slot = swap(shifted), swap(slot2)
    encoded = exchange(encoded, FEATURES)
    packed, part = call(
        decode_kernel,
        (HERE,) * 7,
        [(HERE, spec(rows // 2, LANES, dtype=F32)), (HERE, spec(rows, width))],
        (encoded, slot, slot2, bias_row, bias_row2, weight, weight2),
        [pltpu.VMEM((2, rows, latents), BF16)],
        flops,
        moved,
        MOST,
    )
    part, packed = lax.optimization_barrier((part, packed))
    codes, codes2 = call(
        codes_kernel,
        (HERE,) * 5,
        [(HERE, spec(rows, latents)), (HERE, spec(rows, latents))],
        (packed, swap(packed), slot, other_slot, bias_row),
    )
    parts, codes, codes2, shifted2, other_slot = lax.optimization_barrier(
        (exchange(part.reshape(shares), COLUMN), codes, codes2, shifted2, other_slot)
    )
    (out,) = call(
        error_kernel,
        (SCALARS, HERE, HERE, HERE),
        [(HERE, all_shares)],
        (at, parts, decoder_bias, whitened),
        vmem=SMALL,
    )
    out, weight, weight2 = lax.optimization_barrier((out, decoder_weight, decoder_weight2))
    weight, weight2 = swap(weight2), swap(weight)
    grad = exchange(out, COLUMN).reshape(rows, width)

    packed = chosen_product(1, grad, weight, weight2)
    packed, grad = lax.optimization_barrier((packed, grad))
    (decoder_grad,) = call(
        decoder_grad_kernel,
        (HERE,) * 4,
        [(HERE, spec(latents, width))],
        (codes, codes2, grad, swap(grad)),
        (),
        flops,
        moved,
    )
    code_grad, decoder_grad = lax.optimization_barrier(
        (exchange(packed, FEATURES), decoder_grad)
    )
    code_grad2 = swap(code_grad)
    bias_half = spec(1, latents // 2, dtype=F32)
    first_grad, first_bias = call(
        first_grad_kernel,
        (SCALARS, HERE, HERE, HERE),
        [(HERE, spec(width, latents, dtype=F32)), (HERE, bias_half)],
        (at, code_grad, slot, shifted),
        [pltpu.VMEM((rows, latents), BF16)],
        flops,
        moved,
        MIDDLE,
    )
    encoder_grad, bias_grad = call(
        second_grad_kernel,
        (SCALARS, HERE, HERE, HERE, HERE, HERE),
        [(ANY, spec(width, latents)), (HERE, bias_half)],
        (at, code_grad2, other_slot, shifted2, first_grad, first_bias),
        [
            pltpu.VMEM((rows, latents), BF16),
            pltpu.VMEM((width, latents), BF16),
            COPIES((ROW_BLOCKS,)),
        ],
        flops,
        moved,
        MIDDLE,
    )
    return encoder_grad, decoder_grad, bias_grad[0]


def solution(mesh):
    fine = Mesh(mesh.devices.reshape(4, 2, 8, 2, 2), ("section", "yh", "z", "core", "tok"))
    lat = ("yh", "z", "core")
    return jax.shard_map(
        body,
        mesh=fine,
        in_specs=(
            P("tok", "section", lat),
            P(lat),
            P(lat, "section"),
            P("section"),
            P(("section", "tok"), lat),
            P(lat),
            P(lat, ("section", "tok")),
            P(),
        ),
        out_specs=(P(("section", "tok"), lat), P(lat, ("section", "tok")), P(lat + ("tok",))),
        check_vma=False,
    )
```

```python
import functools

import jax
import jax.numpy as jnp
from jax import lax
from jax.experimental import pallas as pl
from jax.experimental.pallas import tpu as pltpu
from jax.sharding import Mesh
from jax.sharding import PartitionSpec as P

grad_scale = 0.125
LANES = 128
F32 = jnp.float32
BF16 = jnp.bfloat16
HERE = pl.BlockSpec(memory_space=pltpu.VMEM)
SCALARS = pl.BlockSpec(memory_space=pltpu.SMEM)
ANY = pl.BlockSpec(memory_space=pl.ANY)
HBM = pl.BlockSpec(memory_space=pltpu.HBM)
MIB = 1024 * 1024
SMALL, MIDDLE, MOST = 12, 24, 24
COPIES = pltpu.SemaphoreType.DMA
ROW_BLOCKS = 8
EARLY_ROWS = 32
FEATURES = ("section", "tok")
COLUMN = ("yh", "z")
CORE, TOK, FIRST, FIRST2 = range(4)


def spec(*shape, dtype=BF16):
    return jax.ShapeDtypeStruct(shape, dtype)


def call(kernel, ins, outs, operands, scratch=(), flops=0, moved=2**20, vmem=60):
    return pl.pallas_call(
        kernel,
        in_specs=list(ins),
        out_specs=tuple(place for place, _ in outs),
        out_shape=tuple(shape for _, shape in outs),
        scratch_shapes=list(scratch),
        compiler_params=pltpu.CompilerParams(vmem_limit_bytes=vmem * MIB),
        cost_estimate=pl.CostEstimate(flops=flops, bytes_accessed=moved, transcendentals=0),
    )(*operands)


def start(source, target, sem):
    copy = pltpu.make_async_copy(source, target, sem)
    copy.start()
    return copy


def place_kernel(latents, at_ref, chosen_ref, packed_ref, wide_ref):
    picked = chosen_ref[at_ref[CORE]]
    own, other = picked - at_ref[FIRST], picked - at_ref[FIRST2]
    wide_ref[...] = jnp.concatenate([own, other], axis=1)
    place = jnp.where((other >= 0) & (other < latents), other + latents, -1)
    place = jnp.where((own >= 0) & (own < latents), own, place)
    half = place.shape[0] // 2
    packed_ref[...] = jnp.concatenate([place[:half], place[half:]], axis=1)


def find_kernel(done, wide_ref, *refs):
    given, (slot_ref, slot2_ref, found) = refs[:-3], refs[-3:]
    rows, width = slot_ref.shape
    half, picks = wide_ref.shape[0] // 2, LANES // 2
    column = lax.broadcasted_iota(jnp.int32, (8, width), 1)

    def step(base, i, carry):
        own = pl.ds(pl.multiple_of(i * 8, 8), 8)
        place = wide_ref[own, :]
        for n in range(2):
            slot = jnp.full((8, width), -1, jnp.int32)
            for k in range(picks):
                at = n * picks + k
                slot = jnp.where(place[:, at : at + 1] == column, base + k, slot)
            found[n, own, :] = slot
        return carry

    def pack(i, carry):
        own = pl.ds(pl.multiple_of(i * 16, 16), 16)
        for n, out in enumerate((slot_ref, slot2_ref)):
            out[own, :] = found[n, own, :].astype(F32).astype(BF16)
        return carry

    for before, out in zip(given, (slot_ref, slot2_ref)):
        out[:done, :] = before[...]
    lax.fori_loop(done // 8, min(rows, half) // 8, functools.partial(step, 0), 0)
    if rows > half:
        lax.fori_loop(half // 8, rows // 8, functools.partial(step, picks), 0)
    lax.fori_loop(done // 16, rows // 16, pack, 0)


def pick(low, high, place, chunk, j, y):
    half = place.shape[0]
    here = chunk == j
    low = jnp.where(here, jnp.take_along_axis(y[:half], place, axis=1), low)
    high = jnp.where(here, jnp.take_along_axis(y[half:], place, axis=1), high)
    return low, high


def spread(packed, slot, cols):
    lane = slot[:, cols].astype(F32).astype(jnp.int32)
    half = packed.shape[0]
    value = jnp.concatenate(
        [
            jnp.take_along_axis(packed, jnp.maximum(lane[:half], 0), axis=1),
            jnp.take_along_axis(packed, jnp.maximum(lane[half:], 0), axis=1),
        ],
        axis=0,
    )
    return value, lane >= 0


def sum_of(parts_ref):
    total = parts_ref[0].astype(F32)
    for i in range(1, parts_ref.shape[0]):
        total = total + parts_ref[i].astype(F32)
    return total


def whiten_kernel(x_ref, w_ref, x2_ref, w2_ref, out_ref, ready, sems):
    y = jnp.dot(x_ref[...], w_ref[...], preferred_element_type=F32)
    y = y + jnp.dot(x2_ref[...], w2_ref[...], preferred_element_type=F32)
    ready[...] = y.astype(BF16)
    start(ready, out_ref, sems.at[0]).wait()


def own_bias(at_ref, bias_ref, width):
    return bias_ref[:, pl.ds(pl.multiple_of(at_ref[TOK] * width, width), width)]


def shift_kernel(at_ref, parts_ref, bias_ref, white_ref, out_ref):
    white = sum_of(parts_ref).astype(BF16)
    white_ref[...] = white
    shifted = (white.astype(F32) - own_bias(at_ref, bias_ref, white.shape[1])).astype(BF16)
    for i in range(out_ref.shape[0]):
        out_ref[i] = shifted


def error_kernel(at_ref, parts_ref, bias_ref, white_ref, out_ref):
    rebuilt = sum_of(parts_ref) + own_bias(at_ref, bias_ref, white_ref.shape[1])
    grad = (grad_scale * (rebuilt - white_ref[...].astype(F32))).astype(BF16)
    for i in range(out_ref.shape[0]):
        out_ref[i] = grad


def product_kernel(contract, x_ref, place_ref, w_ref, w2_ref, out_ref):
    place = place_ref[...]
    lane, chunk = place & (LANES - 1), place >> 7
    low = high = jnp.zeros(place.shape, F32)
    for n, weight in enumerate((w_ref, w2_ref)):
        y = lax.dot_general(
            x_ref[...], weight[...], (((1,), (contract,)), ((), ())), preferred_element_type=F32
        )
        blocks = y.shape[1] // LANES
        for j in range(blocks):
            part = y[:, j * LANES : (j + 1) * LANES]
            low, high = pick(low, high, lane, chunk, n * blocks + j, part)
    column = lax.broadcasted_iota(jnp.int32, place.shape, 1)
    packed = jnp.where(column < LANES // 2, low, high).astype(BF16)
    for i in range(out_ref.shape[0]):
        out_ref[i] = packed


def spread_codes(packed, slot, bias_ref, codes_ref):
    for j in range(codes_ref.shape[1] // LANES):
        cols = pl.ds(j * LANES, LANES)
        value, there = spread(packed, slot, cols)
        codes_ref[:, cols] = jnp.where(there, value + bias_ref[:, cols], 0.0).astype(BF16)


def decode_kernel(
    parts_ref, slot_ref, slot2_ref, bias_ref, bias2_ref, w_ref, w2_ref, packed_ref, out_ref, codes
):
    packed = sum_of(parts_ref)
    packed_ref[...] = packed
    spread_codes(packed, slot_ref, bias_ref, codes.at[0])
    spread_codes(packed, slot2_ref, bias2_ref, codes.at[1])
    y = jnp.dot(codes[0], w_ref[...], preferred_element_type=F32)
    y = y + jnp.dot(codes[1], w2_ref[...], preferred_element_type=F32)
    out_ref[...] = y.astype(BF16)


ROWS_BY_ROWS = (((0,), (0,)), ((), ()))


def codes_kernel(packed_ref, packed2_ref, slot_ref, slot2_ref, bias_ref, out_ref, out2_ref):
    spread_codes(packed_ref[...], slot_ref, bias_ref, out_ref)
    spread_codes(packed2_ref[...], slot2_ref, bias_ref, out2_ref)


def decoder_grad_kernel(codes_ref, codes2_ref, grad_ref, grad2_ref, out_ref):
    y = lax.dot_general(codes_ref[...], grad_ref[...], ROWS_BY_ROWS, preferred_element_type=F32)
    y = y + lax.dot_general(
        codes2_ref[...], grad2_ref[...], ROWS_BY_ROWS, preferred_element_type=F32
    )
    out_ref[...] = y.astype(BF16)


def spread_grad(parts_ref, slot_ref, grad):
    packed = sum_of(parts_ref)
    for j in range(grad.shape[1] // LANES):
        cols = pl.ds(j * LANES, LANES)
        value, there = spread(packed, slot_ref, cols)
        grad[:, cols] = jnp.where(there, value, 0.0).astype(BF16)


def row_sum(at_ref, grad, kept):
    ones = jnp.ones((16, grad.shape[0]), BF16)
    cols = pl.ds(pl.multiple_of(at_ref[TOK] * kept, kept), kept)
    return jnp.dot(ones, grad[:, cols], preferred_element_type=F32)[:1]


def first_grad_kernel(at_ref, parts_ref, slot_ref, x_ref, out_ref, bias_ref, grad):
    spread_grad(parts_ref, slot_ref, grad)
    bias_ref[...] = row_sum(at_ref, grad, bias_ref.shape[1])
    out_ref[...] = lax.dot_general(
        x_ref[...], grad[...], ROWS_BY_ROWS, preferred_element_type=F32
    )


def second_grad_kernel(
    at_ref, parts_ref, slot_ref, x_ref, first_ref, first_bias_ref, out_ref, bias_ref, grad, made, sems
):
    spread_grad(parts_ref, slot_ref, grad)
    bias_ref[...] = first_bias_ref[...] + row_sum(at_ref, grad, bias_ref.shape[1])
    height = made.shape[0] // ROW_BLOCKS
    copies = []
    for b in range(ROW_BLOCKS):
        own = pl.ds(b * height, height)
        y = lax.dot_general(x_ref[:, own], grad[...], ROWS_BY_ROWS, preferred_element_type=F32)
        made[own, :] = (y + first_ref[own, :]).astype(BF16)
        copies.append(start(made.at[own], out_ref.at[own], sems.at[b]))
    for copy in copies:
        copy.wait()


def swap(x):
    return lax.ppermute(x, "core", [(0, 1), (1, 0)])


def exchange(x, axes):
    return lax.all_to_all(x, axes, 0, 0)


def body(
    residual, center, whiten, decoder_bias, encoder_weight, encoder_bias, decoder_weight, chosen
):
    core = lax.axis_index("core")
    width = encoder_weight.shape[0]
    latents = encoder_bias.shape[0]
    rows, picks = chosen.shape[1:]
    inputs = center.shape[0]
    receivers = lax.axis_size(FEATURES)
    column = lax.axis_size(COLUMN)
    chip = (lax.axis_index("yh") * lax.axis_size("z") + lax.axis_index("z")) * 2
    at = jnp.stack(
        [core, lax.axis_index("tok"), (chip + core) * latents, (chip + 1 - core) * latents]
    ).astype(jnp.int32)

    centered = (residual[0].astype(F32) - center).astype(BF16)
    out = jnp.broadcast_to(centered[None], (receivers,) + centered.shape)
    whiten_cols = lax.dynamic_slice_in_dim(whiten, at[TOK] * width, width, 1)
    out, listed, whiten_cols = lax.optimization_barrier((out, chosen, whiten_cols))
    place, wide = call(
        functools.partial(place_kernel, latents),
        (SCALARS, HERE),
        [
            (HERE, spec(rows // 2, LANES, dtype=jnp.int32)),
            (HERE, spec(rows, LANES, dtype=jnp.int32)),
        ],
        (at, listed),
        vmem=SMALL,
    )

    def find(done, count, operands):
        return call(
            functools.partial(find_kernel, done),
            (HERE,) * len(operands),
            [(HERE, spec(count, latents))] * 2,
            operands,
            [pltpu.VMEM((2, count, latents), jnp.int32)],
            4 * picks * (count - done) * latents,
        )

    early = find(0, EARLY_ROWS, (wide,))
    whiten_cols2 = swap(whiten_cols)
    arrived, wide, place, early = lax.optimization_barrier(
        (exchange(out, ("tok", "section")), wide, place, early)
    )
    arrived = arrived.reshape(2, rows, inputs)
    own_rows = lax.dynamic_index_in_dim(arrived, core, 0, keepdims=False)
    other_rows = lax.dynamic_index_in_dim(arrived, 1 - core, 0, keepdims=False)
    (part,) = call(
        whiten_kernel,
        (HERE,) * 4,
        [(HBM, spec(rows, width))],
        (own_rows, whiten_cols, swap(other_rows), whiten_cols2),
        [pltpu.VMEM((rows, width), BF16), COPIES((1,))],
        4 * rows * width * inputs,
        vmem=SMALL,
    )
    shares = (column, rows // column, width)
    share, all_shares = spec(*shares[1:]), spec(*shares)
    bias_row, decoder_bias = encoder_bias[None], decoder_bias[None]

    part, wide, encoder_weight, decoder_weight, bias_row = lax.optimization_barrier(
        (part, wide, encoder_weight, decoder_weight, bias_row)
    )
    encoder_weight2, decoder_weight2 = swap(encoder_weight), swap(decoder_weight)
    bias_row2 = swap(bias_row)
    slot, slot2 = find(EARLY_ROWS, rows, (wide, *early))
    parts, slot, slot2, bias_row2 = lax.optimization_barrier(
        (exchange(part.reshape(shares), COLUMN), slot, slot2, bias_row2)
    )
    whitened, out = call(
        shift_kernel,
        (SCALARS, HERE, HERE),
        [(HERE, share), (HERE, all_shares)],
        (at, parts, decoder_bias),
        vmem=SMALL,
    )
    out, weight, weight2, later, later2 = lax.optimization_barrier(
        (out, encoder_weight, encoder_weight2, decoder_weight, decoder_weight2)
    )
    weight, weight2 = swap(weight2), swap(weight)
    later, later2 = swap(later2), swap(later)
    shifted = exchange(out, COLUMN).reshape(rows, width)

    flops = 4 * rows * width * latents
    moved = 4 * width * latents

    def chosen_product(contract, x, weight, weight2):
        (packed,) = call(
            functools.partial(product_kernel, contract),
            (HERE, HERE, HERE, HERE),
            [(HERE, spec(receivers, rows // 2, LANES))],
            (x, place, weight, weight2),
            (),
            flops,
            moved,
            MOST,
        )
        return packed

    encoded = chosen_product(0, shifted, weight, weight2)
    encoded, shifted, weight, weight2 = lax.optimization_barrier((encoded, shifted, later, later2))
    shifted2, other_slot = swap(shifted), swap(slot2)
    encoded = exchange(encoded, FEATURES)
    packed, part = call(
        decode_kernel,
        (HERE,) * 7,
        [(HERE, spec(rows // 2, LANES, dtype=F32)), (HERE, spec(rows, width))],
        (encoded, slot, slot2, bias_row, bias_row2, weight, weight2),
        [pltpu.VMEM((2, rows, latents), BF16)],
        flops,
        moved,
        MOST,
    )
    part, packed = lax.optimization_barrier((part, packed))
    codes, codes2 = call(
        codes_kernel,
        (HERE,) * 5,
        [(HERE, spec(rows, latents)), (HERE, spec(rows, latents))],
        (packed, swap(packed), slot, other_slot, bias_row),
    )
    parts, codes, codes2, shifted2, other_slot = lax.optimization_barrier(
        (exchange(part.reshape(shares), COLUMN), codes, codes2, shifted2, other_slot)
    )
    (out,) = call(
        error_kernel,
        (SCALARS, HERE, HERE, HERE),
        [(HERE, all_shares)],
        (at, parts, decoder_bias, whitened),
        vmem=SMALL,
    )
    grad = exchange(out, COLUMN).reshape(rows, width)

    packed = chosen_product(1, grad, weight, weight2)
    packed, grad = lax.optimization_barrier((packed, grad))
    (decoder_grad,) = call(
        decoder_grad_kernel,
        (HERE,) * 4,
        [(HERE, spec(latents, width))],
        (codes, codes2, grad, swap(grad)),
        (),
        flops,
        moved,
    )
    code_grad, decoder_grad = lax.optimization_barrier(
        (exchange(packed, FEATURES), decoder_grad)
    )
    code_grad2 = swap(code_grad)
    bias_half = spec(1, latents // 2, dtype=F32)
    first_grad, first_bias = call(
        first_grad_kernel,
        (SCALARS, HERE, HERE, HERE),
        [(HERE, spec(width, latents, dtype=F32)), (HERE, bias_half)],
        (at, code_grad, slot, shifted),
        [pltpu.VMEM((rows, latents), BF16)],
        flops,
        moved,
        MIDDLE,
    )
    encoder_grad, bias_grad = call(
        second_grad_kernel,
        (SCALARS, HERE, HERE, HERE, HERE, HERE),
        [(ANY, spec(width, latents)), (HERE, bias_half)],
        (at, code_grad2, other_slot, shifted2, first_grad, first_bias),
        [
            pltpu.VMEM((rows, latents), BF16),
            pltpu.VMEM((width, latents), BF16),
            COPIES((ROW_BLOCKS,)),
        ],
        flops,
        moved,
        MIDDLE,
    )
    return encoder_grad, decoder_grad, bias_grad[0]


def solution(mesh):
    fine = Mesh(mesh.devices.reshape(4, 2, 8, 2, 2), ("section", "yh", "z", "core", "tok"))
    lat = ("yh", "z", "core")
    return jax.shard_map(
        body,
        mesh=fine,
        in_specs=(
            P("tok", "section", lat),
            P(lat),
            P(lat, "section"),
            P("section"),
            P(("section", "tok"), lat),
            P(lat),
            P(lat, ("section", "tok")),
            P(),
        ),
        out_specs=(P(("section", "tok"), lat), P(lat, ("section", "tok")), P(lat + ("tok",))),
        check_vma=False,
    )
```

```python
import functools

import jax
import jax.numpy as jnp
from jax import lax
from jax.experimental import pallas as pl
from jax.experimental.pallas import tpu as pltpu
from jax.sharding import Mesh
from jax.sharding import PartitionSpec as P

grad_scale = 0.125
LANES = 128
F32 = jnp.float32
BF16 = jnp.bfloat16
HERE = pl.BlockSpec(memory_space=pltpu.VMEM)
SCALARS = pl.BlockSpec(memory_space=pltpu.SMEM)
ANY = pl.BlockSpec(memory_space=pl.ANY)
HBM = pl.BlockSpec(memory_space=pltpu.HBM)
MIB = 1024 * 1024
SMALL, MIDDLE, MOST = 12, 24, 24
COPIES = pltpu.SemaphoreType.DMA
ROW_BLOCKS = 8
EARLY_ROWS = 16
FEATURES = ("section", "tok")
COLUMN = ("yh", "z")
CORE, TOK, FIRST, FIRST2 = range(4)


def spec(*shape, dtype=BF16):
    return jax.ShapeDtypeStruct(shape, dtype)


def call(kernel, ins, outs, operands, scratch=(), flops=0, moved=2**20, vmem=60):
    return pl.pallas_call(
        kernel,
        in_specs=list(ins),
        out_specs=tuple(place for place, _ in outs),
        out_shape=tuple(shape for _, shape in outs),
        scratch_shapes=list(scratch),
        compiler_params=pltpu.CompilerParams(vmem_limit_bytes=vmem * MIB),
        cost_estimate=pl.CostEstimate(flops=flops, bytes_accessed=moved, transcendentals=0),
    )(*operands)


def start(source, target, sem):
    copy = pltpu.make_async_copy(source, target, sem)
    copy.start()
    return copy


def place_kernel(latents, at_ref, chosen_ref, packed_ref, wide_ref):
    picked = chosen_ref[at_ref[CORE]]
    own, other = picked - at_ref[FIRST], picked - at_ref[FIRST2]
    wide_ref[...] = jnp.concatenate([own, other], axis=1)
    place = jnp.where((other >= 0) & (other < latents), other + latents, -1)
    place = jnp.where((own >= 0) & (own < latents), own, place)
    half = place.shape[0] // 2
    packed_ref[...] = jnp.concatenate([place[:half], place[half:]], axis=1)


def find_kernel(done, wide_ref, *refs):
    given, (slot_ref, slot2_ref, found) = refs[:-3], refs[-3:]
    rows, width = slot_ref.shape
    half, picks = wide_ref.shape[0] // 2, LANES // 2
    column = lax.broadcasted_iota(jnp.int32, (8, width), 1)

    def step(base, i, carry):
        own = pl.ds(pl.multiple_of(i * 8, 8), 8)
        place = wide_ref[own, :]
        for n in range(2):
            slot = jnp.full((8, width), -1, jnp.int32)
            for k in range(picks):
                at = n * picks + k
                slot = jnp.where(place[:, at : at + 1] == column, base + k, slot)
            found[n, own, :] = slot
        return carry

    def pack(i, carry):
        own = pl.ds(pl.multiple_of(i * 16, 16), 16)
        for n, out in enumerate((slot_ref, slot2_ref)):
            out[own, :] = found[n, own, :].astype(F32).astype(BF16)
        return carry

    for before, out in zip(given, (slot_ref, slot2_ref)):
        out[:done, :] = before[...]
    lax.fori_loop(done // 8, min(rows, half) // 8, functools.partial(step, 0), 0)
    if rows > half:
        lax.fori_loop(half // 8, rows // 8, functools.partial(step, picks), 0)
    lax.fori_loop(done // 16, rows // 16, pack, 0)


def pick(low, high, place, chunk, j, y):
    half = place.shape[0]
    here = chunk == j
    low = jnp.where(here, jnp.take_along_axis(y[:half], place, axis=1), low)
    high = jnp.where(here, jnp.take_along_axis(y[half:], place, axis=1), high)
    return low, high


def spread(packed, slot, cols):
    lane = slot[:, cols].astype(F32).astype(jnp.int32)
    half = packed.shape[0]
    value = jnp.concatenate(
        [
            jnp.take_along_axis(packed, jnp.maximum(lane[:half], 0), axis=1),
            jnp.take_along_axis(packed, jnp.maximum(lane[half:], 0), axis=1),
        ],
        axis=0,
    )
    return value, lane >= 0


def sum_of(parts_ref):
    total = parts_ref[0].astype(F32)
    for i in range(1, parts_ref.shape[0]):
        total = total + parts_ref[i].astype(F32)
    return total


def whiten_kernel(x_ref, w_ref, x2_ref, w2_ref, out_ref, ready, sems):
    y = jnp.dot(x_ref[...], w_ref[...], preferred_element_type=F32)
    y = y + jnp.dot(x2_ref[...], w2_ref[...], preferred_element_type=F32)
    ready[...] = y.astype(BF16)
    start(ready, out_ref, sems.at[0]).wait()


def own_bias(at_ref, bias_ref, width):
    return bias_ref[:, pl.ds(pl.multiple_of(at_ref[TOK] * width, width), width)]


def shift_kernel(at_ref, parts_ref, bias_ref, white_ref, out_ref):
    white = sum_of(parts_ref).astype(BF16)
    white_ref[...] = white
    shifted = (white.astype(F32) - own_bias(at_ref, bias_ref, white.shape[1])).astype(BF16)
    for i in range(out_ref.shape[0]):
        out_ref[i] = shifted


def error_kernel(at_ref, parts_ref, bias_ref, white_ref, out_ref):
    rebuilt = sum_of(parts_ref) + own_bias(at_ref, bias_ref, white_ref.shape[1])
    grad = (grad_scale * (rebuilt - white_ref[...].astype(F32))).astype(BF16)
    for i in range(out_ref.shape[0]):
        out_ref[i] = grad


def product_kernel(contract, x_ref, place_ref, w_ref, w2_ref, out_ref):
    place = place_ref[...]
    lane, chunk = place & (LANES - 1), place >> 7
    low = high = jnp.zeros(place.shape, F32)
    for n, weight in enumerate((w_ref, w2_ref)):
        y = lax.dot_general(
            x_ref[...], weight[...], (((1,), (contract,)), ((), ())), preferred_element_type=F32
        )
        blocks = y.shape[1] // LANES
        for j in range(blocks):
            part = y[:, j * LANES : (j + 1) * LANES]
            low, high = pick(low, high, lane, chunk, n * blocks + j, part)
    column = lax.broadcasted_iota(jnp.int32, place.shape, 1)
    packed = jnp.where(column < LANES // 2, low, high).astype(BF16)
    for i in range(out_ref.shape[0]):
        out_ref[i] = packed


def spread_codes(packed, slot, bias_ref, codes_ref):
    for j in range(codes_ref.shape[1] // LANES):
        cols = pl.ds(j * LANES, LANES)
        value, there = spread(packed, slot, cols)
        codes_ref[:, cols] = jnp.where(there, value + bias_ref[:, cols], 0.0).astype(BF16)


def decode_kernel(
    parts_ref, slot_ref, slot2_ref, bias_ref, bias2_ref, w_ref, w2_ref, packed_ref, out_ref, codes
):
    packed = sum_of(parts_ref)
    packed_ref[...] = packed
    spread_codes(packed, slot_ref, bias_ref, codes.at[0])
    spread_codes(packed, slot2_ref, bias2_ref, codes.at[1])
    y = jnp.dot(codes[0], w_ref[...], preferred_element_type=F32)
    y = y + jnp.dot(codes[1], w2_ref[...], preferred_element_type=F32)
    out_ref[...] = y.astype(BF16)


ROWS_BY_ROWS = (((0,), (0,)), ((), ()))


def codes_kernel(packed_ref, packed2_ref, slot_ref, slot2_ref, bias_ref, out_ref, out2_ref):
    spread_codes(packed_ref[...], slot_ref, bias_ref, out_ref)
    spread_codes(packed2_ref[...], slot2_ref, bias_ref, out2_ref)


def decoder_grad_kernel(codes_ref, codes2_ref, grad_ref, grad2_ref, out_ref):
    y = lax.dot_general(codes_ref[...], grad_ref[...], ROWS_BY_ROWS, preferred_element_type=F32)
    y = y + lax.dot_general(
        codes2_ref[...], grad2_ref[...], ROWS_BY_ROWS, preferred_element_type=F32
    )
    out_ref[...] = y.astype(BF16)


def spread_grad(parts_ref, slot_ref, grad):
    packed = sum_of(parts_ref)
    for j in range(grad.shape[1] // LANES):
        cols = pl.ds(j * LANES, LANES)
        value, there = spread(packed, slot_ref, cols)
        grad[:, cols] = jnp.where(there, value, 0.0).astype(BF16)


def row_sum(at_ref, grad, kept):
    ones = jnp.ones((16, grad.shape[0]), BF16)
    cols = pl.ds(pl.multiple_of(at_ref[TOK] * kept, kept), kept)
    return jnp.dot(ones, grad[:, cols], preferred_element_type=F32)[:1]


def first_grad_kernel(at_ref, parts_ref, slot_ref, x_ref, out_ref, bias_ref, grad):
    spread_grad(parts_ref, slot_ref, grad)
    bias_ref[...] = row_sum(at_ref, grad, bias_ref.shape[1])
    out_ref[...] = lax.dot_general(
        x_ref[...], grad[...], ROWS_BY_ROWS, preferred_element_type=F32
    )


def second_grad_kernel(
    at_ref, parts_ref, slot_ref, x_ref, first_ref, first_bias_ref, out_ref, bias_ref, grad, made, sems
):
    spread_grad(parts_ref, slot_ref, grad)
    bias_ref[...] = first_bias_ref[...] + row_sum(at_ref, grad, bias_ref.shape[1])
    height = made.shape[0] // ROW_BLOCKS
    copies = []
    for b in range(ROW_BLOCKS):
        own = pl.ds(b * height, height)
        y = lax.dot_general(x_ref[:, own], grad[...], ROWS_BY_ROWS, preferred_element_type=F32)
        made[own, :] = (y + first_ref[own, :]).astype(BF16)
        copies.append(start(made.at[own], out_ref.at[own], sems.at[b]))
    for copy in copies:
        copy.wait()


def swap(x):
    return lax.ppermute(x, "core", [(0, 1), (1, 0)])


def exchange(x, axes):
    return lax.all_to_all(x, axes, 0, 0)


def body(
    residual, center, whiten, decoder_bias, encoder_weight, encoder_bias, decoder_weight, chosen
):
    core = lax.axis_index("core")
    width = encoder_weight.shape[0]
    latents = encoder_bias.shape[0]
    rows, picks = chosen.shape[1:]
    inputs = center.shape[0]
    receivers = lax.axis_size(FEATURES)
    column = lax.axis_size(COLUMN)
    chip = (lax.axis_index("yh") * lax.axis_size("z") + lax.axis_index("z")) * 2
    at = jnp.stack(
        [core, lax.axis_index("tok"), (chip + core) * latents, (chip + 1 - core) * latents]
    ).astype(jnp.int32)

    centered = (residual[0].astype(F32) - center).astype(BF16)
    out = jnp.broadcast_to(centered[None], (receivers,) + centered.shape)
    whiten_cols = lax.dynamic_slice_in_dim(whiten, at[TOK] * width, width, 1)
    out, listed, whiten_cols = lax.optimization_barrier((out, chosen, whiten_cols))
    place, wide = call(
        functools.partial(place_kernel, latents),
        (SCALARS, HERE),
        [
            (HERE, spec(rows // 2, LANES, dtype=jnp.int32)),
            (HERE, spec(rows, LANES, dtype=jnp.int32)),
        ],
        (at, listed),
        vmem=SMALL,
    )

    def find(done, count, operands):
        return call(
            functools.partial(find_kernel, done),
            (HERE,) * len(operands),
            [(HERE, spec(count, latents))] * 2,
            operands,
            [pltpu.VMEM((2, count, latents), jnp.int32)],
            4 * picks * (count - done) * latents,
        )

    early = find(0, EARLY_ROWS, (wide,))
    whiten_cols2 = swap(whiten_cols)
    arrived, wide, place, early = lax.optimization_barrier(
        (exchange(out, ("tok", "section")), wide, place, early)
    )
    arrived = arrived.reshape(2, rows, inputs)
    own_rows = lax.dynamic_index_in_dim(arrived, core, 0, keepdims=False)
    other_rows = lax.dynamic_index_in_dim(arrived, 1 - core, 0, keepdims=False)
    (part,) = call(
        whiten_kernel,
        (HERE,) * 4,
        [(HBM, spec(rows, width))],
        (own_rows, whiten_cols, swap(other_rows), whiten_cols2),
        [pltpu.VMEM((rows, width), BF16), COPIES((1,))],
        4 * rows * width * inputs,
        vmem=SMALL,
    )
    shares = (column, rows // column, width)
    share, all_shares = spec(*shares[1:]), spec(*shares)
    bias_row, decoder_bias = encoder_bias[None], decoder_bias[None]

    part, wide, encoder_weight, decoder_weight, bias_row = lax.optimization_barrier(
        (part, wide, encoder_weight, decoder_weight, bias_row)
    )
    encoder_weight2, decoder_weight2 = swap(encoder_weight), swap(decoder_weight)
    bias_row2 = swap(bias_row)
    slot, slot2 = find(EARLY_ROWS, rows, (wide, *early))
    parts, slot, slot2, bias_row2 = lax.optimization_barrier(
        (exchange(part.reshape(shares), COLUMN), slot, slot2, bias_row2)
    )
    whitened, out = call(
        shift_kernel,
        (SCALARS, HERE, HERE),
        [(HERE, share), (HERE, all_shares)],
        (at, parts, decoder_bias),
        vmem=SMALL,
    )
    out, weight, weight2, later, later2 = lax.optimization_barrier(
        (out, encoder_weight, encoder_weight2, decoder_weight, decoder_weight2)
    )
    weight, weight2 = swap(weight2), swap(weight)
    later, later2 = swap(later2), swap(later)
    shifted = exchange(out, COLUMN).reshape(rows, width)

    flops = 4 * rows * width * latents
    moved = 4 * width * latents

    def chosen_product(contract, x, weight, weight2):
        (packed,) = call(
            functools.partial(product_kernel, contract),
            (HERE, HERE, HERE, HERE),
            [(HERE, spec(receivers, rows // 2, LANES))],
            (x, place, weight, weight2),
            (),
            flops,
            moved,
            MOST,
        )
        return packed

    encoded = chosen_product(0, shifted, weight, weight2)
    encoded, shifted, weight, weight2 = lax.optimization_barrier((encoded, shifted, later, later2))
    shifted2, other_slot = swap(shifted), swap(slot2)
    encoded = exchange(encoded, FEATURES)
    packed, part = call(
        decode_kernel,
        (HERE,) * 7,
        [(HERE, spec(rows // 2, LANES, dtype=F32)), (HERE, spec(rows, width))],
        (encoded, slot, slot2, bias_row, bias_row2, weight, weight2),
        [pltpu.VMEM((2, rows, latents), BF16)],
        flops,
        moved,
        MOST,
    )
    part, packed = lax.optimization_barrier((part, packed))
    codes, codes2 = call(
        codes_kernel,
        (HERE,) * 5,
        [(HERE, spec(rows, latents)), (HERE, spec(rows, latents))],
        (packed, swap(packed), slot, other_slot, bias_row),
    )
    parts, codes, codes2, shifted2, other_slot = lax.optimization_barrier(
        (exchange(part.reshape(shares), COLUMN), codes, codes2, shifted2, other_slot)
    )
    (out,) = call(
        error_kernel,
        (SCALARS, HERE, HERE, HERE),
        [(HERE, all_shares)],
        (at, parts, decoder_bias, whitened),
        vmem=SMALL,
    )
    out, weight, weight2 = lax.optimization_barrier((out, decoder_weight, decoder_weight2))
    weight, weight2 = swap(weight2), swap(weight)
    grad = exchange(out, COLUMN).reshape(rows, width)

    packed = chosen_product(1, grad, weight, weight2)
    packed, grad = lax.optimization_barrier((packed, grad))
    (decoder_grad,) = call(
        decoder_grad_kernel,
        (HERE,) * 4,
        [(HERE, spec(latents, width))],
        (codes, codes2, grad, swap(grad)),
        (),
        flops,
        moved,
    )
    code_grad, decoder_grad = lax.optimization_barrier(
        (exchange(packed, FEATURES), decoder_grad)
    )
    code_grad2 = swap(code_grad)
    bias_half = spec(1, latents // 2, dtype=F32)
    first_grad, first_bias = call(
        first_grad_kernel,
        (SCALARS, HERE, HERE, HERE),
        [(HERE, spec(width, latents, dtype=F32)), (HERE, bias_half)],
        (at, code_grad, slot, shifted),
        [pltpu.VMEM((rows, latents), BF16)],
        flops,
        moved,
        MIDDLE,
    )
    encoder_grad, bias_grad = call(
        second_grad_kernel,
        (SCALARS, HERE, HERE, HERE, HERE, HERE),
        [(ANY, spec(width, latents)), (HERE, bias_half)],
        (at, code_grad2, other_slot, shifted2, first_grad, first_bias),
        [
            pltpu.VMEM((rows, latents), BF16),
            pltpu.VMEM((width, latents), BF16),
            COPIES((ROW_BLOCKS,)),
        ],
        flops,
        moved,
        MIDDLE,
    )
    return encoder_grad, decoder_grad, bias_grad[0]


def solution(mesh):
    fine = Mesh(mesh.devices.reshape(4, 2, 8, 2, 2), ("section", "yh", "z", "core", "tok"))
    lat = ("yh", "z", "core")
    return jax.shard_map(
        body,
        mesh=fine,
        in_specs=(
            P("tok", "section", lat),
            P(lat),
            P(lat, "section"),
            P("section"),
            P(("section", "tok"), lat),
            P(lat),
            P(lat, ("section", "tok")),
            P(),
        ),
        out_specs=(P(("section", "tok"), lat), P(lat, ("section", "tok")), P(lat + ("tok",))),
        check_vma=False,
    )
```
